256 devices in a mesh: blk: 64 (over y, z_hi, x, core), head: 4 (over z_lo).
Axes of the slice: x: 4, y: 4, z: 8 (z_hi: 2, z_lo: 4; z = z_hi * 4 + z_lo), core: 2. Of those that a mesh axis runs over, the one named last changes fastest.
Arguments:
- query_in: bfloat16 [8192, 2048], P(('blk', 'head')), may hold values from -6 to 6
- key_in: bfloat16 [8192, 2048], P(('blk', 'head')), may hold values from -6 to 6
- value_in: bfloat16 [8192, 2048], P(('blk', 'head')), may hold values from -6 to 6
- saved_out: bfloat16 [8192, 2048], P(('blk', 'head')), may hold values from -0.59765625 to 0.59765625
- grad_out: bfloat16 [8192, 2048], P(('blk', 'head')), may hold values from -6 to 6
- saved_lse: float32 [8192, 16], P('blk', 'head'), may hold values from 3 to 6
- row_block: int32 [8192], replicated, may hold values from 0 to 15, as said below
- row_copy: int32 [8192], replicated, may hold values from 0 to 1, as said below
Outputs:
- grad_query: bfloat16 [8192, 2048], P(('blk', 'head'))
- grad_key: bfloat16 [8192, 2048], P(('blk', 'head'))
- grad_value: bfloat16 [8192, 2048], P(('blk', 'head'))
The draws below stay inside these ranges and needn't reach their ends.
Inputs may be any that keep to these rules, and one draw needn't show every extreme that they name: `row_block`: rows g * 2 * 256 to (g + 1) * 2 * 256 - 1 all carry one block id, and each of the 16 ids is carried by exactly one such run. `row_copy`: in each aligned run of 128 rows exactly 64 rows are 1.
All inputs are finite; a program needn't handle non-finite values.
Results may differ from the reference program's by a relative error of at most 0.0085.
Values may be sent and summed in bfloat16 or wider, within the bound.
No kernel may reach another device: no remote copies, remote signals or barrier semaphores. Data moves between devices by JAX's collectives and lax.ppermute only.
A program may use at most 192 MiB of HBM per device.

```python
import jax
import jax.numpy as jnp
from jax import lax

HEADS = 16
HD = 128
BLOCK = 256
SHARD_ROWS = 128
ROWS = 8192
BLOCKS = 16


def draw_row_block(key, part):
    key = jax.random.fold_in(key, 11)
    block_order = jax.random.permutation(key, BLOCKS)
    return jnp.repeat(block_order, 2 * BLOCK, total_repeat_length=ROWS).astype(jnp.int32)


def draw_row_copy(key, part):
    key = jax.random.fold_in(key, 23)
    shard_keys = jax.random.split(key, ROWS // SHARD_ROWS)
    arranged = jax.vmap(lambda sub_key: jax.random.permutation(sub_key, SHARD_ROWS))(shard_keys)
    return (arranged >= SHARD_ROWS // 2).astype(jnp.int32).reshape(ROWS)


def levels(rng, dims, cuts, least, largest):
    factor_of, own = 1.0, jax.random.fold_in(rng, 6)
    for dim, parts in cuts:
        draws = jnp.exp(jax.random.uniform(jax.random.fold_in(own, dim), (parts,), jnp.float32, least / len(cuts), largest / len(cuts)))
        factor_of = factor_of * jnp.repeat(draws, dims[dim] // parts).reshape([-1 if axis == dim else 1 for axis in range(len(dims))])
    return factor_of


def noise(rng, dims, deviation, bound, pieces=(), held_as=jnp.bfloat16):
    entries = deviation * jax.random.normal(rng, dims, jnp.float32)
    if pieces:
        entries = entries * levels(rng, dims, pieces, -0.22, 0.18)
    return jnp.clip(entries, -bound, bound).astype(held_as)


def setup_inputs(seed: int = 0) -> dict:
    splits = jax.random.split(jax.random.key(seed), 9)
    return {
        "query_in": noise(splits[0], (ROWS, HEADS * HD), 1.0, 6.0, ((0, 256),)),
        "key_in": noise(splits[1], (ROWS, HEADS * HD), 1.0, 6.0, ((0, 256),)),
        "value_in": noise(splits[2], (ROWS, HEADS * HD), 1.0, 6.0, ((0, 256),)),
        "saved_out": noise(splits[3], (ROWS, HEADS * HD), 0.1, 0.59765625, ((0, 256),)),
        "grad_out": noise(splits[4], (ROWS, HEADS * HD), 1.0, 6.0, ((0, 256),)),
        "saved_lse": jnp.clip(3.0 + 3.0 * jax.random.uniform(splits[5], (ROWS, HEADS), jnp.float32) ** levels(splits[5], (ROWS, HEADS), ((0, 64), (1, 4)), -0.2, 0.2), 3.0, 6.0),
        "row_block": draw_row_block(jax.random.fold_in(splits[8], 71), 0),
        "row_copy": draw_row_copy(jax.random.fold_in(splits[8], 71), 0),
    }


def block_mask(row_block, row_copy):
    query_block = row_block[:, None]
    key_block = row_block[None, :]
    query_copy = row_copy[:, None]
    key_copy = row_copy[None, :]
    clean_part = (key_copy == 1) & ((key_block < query_block) | ((key_block == query_block) & (query_copy == 1)))
    noisy_part = (key_copy == 0) & (query_copy == 0) & (key_block == query_block)
    return clean_part | noisy_part


def reference(query_in, key_in, value_in, saved_out, grad_out, saved_lse, row_block, row_copy):
    allowed = block_mask(row_block, row_copy)
    scaling = HD ** -0.5

    def split_heads(matrix):
        return jnp.transpose(matrix.reshape(ROWS, HEADS, HD), (1, 0, 2))

    row_delta = jnp.sum(grad_out.astype(jnp.float32).reshape(ROWS, HEADS, HD) * saved_out.astype(jnp.float32).reshape(ROWS, HEADS, HD), axis=2)

    def one_head(inputs):
        head_query, head_keys, head_values, head_grad, head_lse, head_delta = inputs
        scores = jnp.dot(head_query, head_keys.T, preferred_element_type=jnp.float32) * scaling
        weights = jnp.where(allowed, jnp.exp(scores - head_lse[:, None]), 0.0)
        weights_low = weights.astype(jnp.bfloat16)
        dweights = jnp.dot(head_grad, head_values.T, preferred_element_type=jnp.float32)
        dscores = (weights * (dweights - head_delta[:, None])).astype(jnp.bfloat16)
        grad_query = (scaling * jnp.dot(dscores, head_keys, preferred_element_type=jnp.float32)).astype(jnp.bfloat16)
        grad_key = (scaling * jnp.dot(dscores.T, head_query, preferred_element_type=jnp.float32)).astype(jnp.bfloat16)
        grad_value = jnp.dot(weights_low.T, head_grad, preferred_element_type=jnp.float32).astype(jnp.bfloat16)
        return grad_query, grad_key, grad_value

    stacked = lax.map(one_head, (split_heads(query_in), split_heads(key_in), split_heads(value_in), split_heads(grad_out), jnp.transpose(saved_lse), jnp.transpose(row_delta)))

    def merge_heads(tensor):
        return jnp.transpose(tensor, (1, 0, 2)).reshape(ROWS, HEADS * HD)

    return merge_heads(stacked[0]), merge_heads(stacked[1]), merge_heads(stacked[2])
```

```python
import functools

import jax
import jax.numpy as jnp
from jax import lax
from jax.experimental import pallas as pl
from jax.experimental.pallas import tpu as pltpu
from jax.sharding import Mesh
from jax.sharding import PartitionSpec as P

HD = 128
RUN = 128
HALF = RUN // 2
AXES = ("y", "zh", "xh", "xl", "c", "zl")
SIZES = (4, 2, 2, 2, 2, 4)
HEAD_AXES = ("zh", "c", "zl")
QUERY_AXES = ("xh", "xl")
KEY_AXES = ("y",)
RUNS = 4
SCALE = HD**-0.5
LOG2E = 1.4426950408889634
F32 = jnp.float32
BF16 = jnp.bfloat16
VMEM = pl.BlockSpec(memory_space=pltpu.VMEM)
SMEM = pl.BlockSpec(memory_space=pltpu.SMEM)


def iota(shape, axis):
    return lax.broadcasted_iota(jnp.int32, shape, axis)


def split_two(x):
    high = x.astype(BF16).astype(F32)
    return high, x - high


def contract(a, b, dim_a, dim_b):
    return lax.dot_general(a, b, (((dim_a,), (dim_b,)), ((), ())), preferred_element_type=F32)


def call(body, out_shape, args, smem=(), scratch=(), limit=32 << 20, cost=None):
    return pl.pallas_call(
        body,
        out_shape=out_shape,
        in_specs=[SMEM if i in smem else VMEM for i in range(len(args))],
        out_specs=jax.tree.map(lambda _: VMEM, out_shape),
        scratch_shapes=list(scratch),
        compiler_params=pltpu.CompilerParams(vmem_limit_bytes=limit),
        cost_estimate=cost,
    )(*args)


def pack_kernel(q_ref, k_ref, v_ref, o_ref, g_ref, lse_ref, out_ref):
    rows = q_ref.shape[0]
    lane = iota((rows, 128), 1)
    delta = jnp.zeros((rows, 128), F32)
    for h in range(16):
        cols = slice(h * HD, (h + 1) * HD)
        term = g_ref[:, cols].astype(F32) * o_ref[:, cols].astype(F32)
        delta = jnp.where(lane == h, jnp.sum(term, axis=1, keepdims=True), delta)
    delta = jnp.concatenate([delta, jnp.zeros((128 - rows, 128), F32)], axis=0).T
    delta_high, delta_low = split_two(delta)
    lse_high, lse_low = split_two(lse_ref[...])
    row = iota((16, 128), 0)
    for slot in range(16):
        j, z = divmod(slot, 4)
        h = 4 * z + j
        cols = slice(h * HD, (h + 1) * HD)
        for i, ref in enumerate((q_ref, g_ref, k_ref, v_ref)):
            out_ref[slot, i * rows : (i + 1) * rows, :] = ref[:, cols]
        stats = jnp.where(row == 0, lse_high[j : j + 1], 0.0)
        stats = jnp.where(row == 1, lse_low[j : j + 1], stats)
        stats = jnp.where(row == 2, delta_high[h : h + 1], stats)
        stats = jnp.where(row == 3, delta_low[h : h + 1], stats)
        out_ref[slot, 4 * rows : 4 * rows + 16, :] = stats.astype(BF16)


def placing(copy_ref, j):
    zh, c = divmod(j, 2)
    shard = ((lax.axis_index("y") * 2 + zh) * 4 + lax.axis_index("xh") * 2 + lax.axis_index("xl")) * 2 + c
    copy = jnp.broadcast_to(copy_ref[pl.ds(shard, 1), :], (8, RUN)).astype(F32)
    upto = (iota((RUN, RUN), 0) <= iota((RUN, RUN), 1)).astype(BF16)
    count = contract(copy.astype(BF16), upto, 1, 0)
    index = iota((8, RUN), 1).astype(F32)
    place = jnp.where(copy > 0.5, HALF - 1.0 + count, index - count)
    place = jnp.broadcast_to(place[0:1], (RUN, RUN)).astype(jnp.int32)
    return (iota((RUN, RUN), 0) == place).astype(F32)


def sort_kernel(got_ref, copy_ref, qd_ref, kv_ref, kvn_ref):
    zl = lax.axis_index("zl")
    row = iota((16, RUN), 0)
    stats = []
    for j in range(RUNS):
        zh, c = divmod(j, 2)
        one_hot = placing(copy_ref, j).astype(BF16)
        parts = [
            jnp.concatenate([got_ref[4 * j + z, 32 * i : 32 * i + 32, :] for z in range(4)], axis=0)
            for i in range(4)
        ]
        moved = contract(one_hot, jnp.concatenate(parts, axis=1), 1, 0).astype(BF16)
        qd_ref[256 * zh + 64 * c : 256 * zh + 64 * c + 64, :] = moved[:HALF, :256]
        qd_ref[256 * zh + 128 + 64 * c : 256 * zh + 192 + 64 * c, :] = moved[HALF:, :256]
        kvn_ref[128 * zh + 64 * c : 128 * zh + 64 * c + 64, :] = moved[:HALF, 256:]
        kv_ref[128 * zh + 64 * c : 128 * zh + 64 * c + 64, :] = moved[HALF:, 256:]
        lse = got_ref[4 * j + zl, 128:144, :].astype(F32)
        delta = jnp.concatenate(
            [got_ref[4 * j + z, 128:144, :].astype(F32)[:, :32] for z in range(4)], axis=1
        )
        both = jnp.where(row < 2, lse, delta).astype(BF16)
        stats.append(contract(both, one_hot, 1, 1))
    halves = []
    for zh in range(2):
        a, b = stats[2 * zh], stats[2 * zh + 1]
        halves.append(
            jnp.concatenate([a[:8, :HALF], b[:8, :HALF], a[:8, HALF:], b[:8, HALF:]], axis=1)
        )
    qd_ref[512:528, :] = jnp.concatenate(halves, axis=0).astype(BF16)


def tile(k, kt, v, q, g, lse, delta):
    scores = contract(k, q, 1, 1)
    weights = jnp.exp2(scores * (SCALE * LOG2E) - lse)
    dweights = contract(v, g, 1, 1)
    dscores = (weights * (dweights - delta)).astype(BF16)
    dv = contract(weights.astype(BF16), g, 1, 0)
    dk = contract(dscores, q, 1, 0)
    dq = contract(kt, dscores, 1, 0)
    return dv, dk, dq


def attend_kernel(
    ids_ref, qd0, qd1, qd2, qd3, kv0, kv1, kv2, kv3, kvn_ref,
    dq0, dq1, dq2, dq3, dkv0, dkv1, dkv2, dkv3, dkvn_ref,
    q_all, g_all, lse_all, delta_all, k_all, kt_all, v_all, dqt, dk_all, dv_all,
):
    y, xh = lax.axis_index("y"), lax.axis_index("xh")
    for m, ref in enumerate((qd0, qd1, qd2, qd3)):
        stats = ref[512:528, :].astype(F32)
        for zh in range(2):
            block, at = zh * 2 + m // 2, 256 * (m % 2)
            q_all[block, at : at + 256, :] = ref[256 * zh : 256 * zh + 256, :HD]
            g_all[block, at : at + 256, :] = ref[256 * zh : 256 * zh + 256, HD:]
            s = 8 * zh
            lse_all[block, :, at : at + 256] = (stats[s : s + 1] + stats[s + 1 : s + 2]) * LOG2E
            delta_all[block, :, at : at + 256] = stats[s + 2 : s + 3] + stats[s + 3 : s + 4]
    for d, ref in enumerate((kv0, kv1, kv2, kv3)):
        for zh in range(2):
            n = 2 * d + zh
            k = ref[128 * zh : 128 * zh + 128, :HD]
            k_all[n] = k
            kt_all[n] = k.astype(F32).T.astype(BF16)
            v_all[n] = ref[128 * zh : 128 * zh + 128, HD:]
    dk_all[...] = jnp.zeros_like(dk_all)
    dv_all[...] = jnp.zeros_like(dv_all)

    for zh in range(2):
        block, n = zh * 2, zh
        kn = kvn_ref[128 * zh : 128 * zh + 128, :HD]
        vn = kvn_ref[128 * zh : 128 * zh + 128, HD:]
        knt = kn.astype(F32).T.astype(BF16)
        for copy in range(2):
            first, second = 128 * copy, 256 + 128 * copy

            def rows(ref):
                return jnp.concatenate([ref[block, first : first + 128, :], ref[block, second : second + 128, :]], axis=0)

            def lanes(ref):
                return jnp.concatenate([ref[block, :, first : first + 128], ref[block, :, second : second + 128]], axis=1)

            q, g, lse, delta = rows(q_all), rows(g_all), lanes(lse_all), lanes(delta_all)
            if copy == 0:
                dv, dk, dq = tile(kn, knt, vn, q, g, lse, delta)
                dkvn_ref[128 * zh : 128 * zh + 128, :] = jnp.concatenate([dk * SCALE, dv], axis=1).astype(BF16)
            else:
                dv, dk, dq = tile(k_all[n], kt_all[n], v_all[n], q, g, lse, delta)
                dk_all[n] = dk
                dv_all[n] = dv
            dqt[block, :, first : first + 128] = dq[:, :128]
            dqt[block, :, second : second + 128] = dq[:, 128:]
    for zh in range(2):
        dqt[zh * 2 + 1] = jnp.zeros((HD, 512), F32)

    for block in range(4):
        zq, other = divmod(block, 2)
        own_id = ids_ref[(y * 2 + zq) * 2 + (xh ^ other)]

        def step(n, carry, block=block, own_id=own_id):
            key_id = ids_ref[((y ^ (n // 2)) * 2 + n % 2) * 2 + xh]

            @pl.when(key_id < own_id)
            def _():
                dv, dk, dq = tile(
                    k_all[n], kt_all[n], v_all[n], q_all[block], g_all[block], lse_all[block], delta_all[block]
                )
                dv_all[n] += dv
                dk_all[n] += dk
                dqt[block] += dq

            return carry

        lax.fori_loop(0, 8, step, 0)

    for m, ref in enumerate((dq0, dq1, dq2, dq3)):
        for zh in range(2):
            block, at = zh * 2 + m // 2, 256 * (m % 2)
            ref[256 * zh : 256 * zh + 256, :] = (dqt[block, :, at : at + 256].T * SCALE).astype(ref.dtype)
    for d, ref in enumerate((dkv0, dkv1, dkv2, dkv3)):
        for zh in range(2):
            n = 2 * d + zh
            ref[128 * zh : 128 * zh + 128, :HD] = (dk_all[n] * SCALE).astype(ref.dtype)
            ref[128 * zh : 128 * zh + 128, HD:] = dv_all[n].astype(ref.dtype)


def unsort_kernel(dq0, dq1, dq2, dq3, dkv0, dkv1, dkv2, dkv3, dkvn_ref, copy_ref, out_ref):
    dq = dq0[...] + dq1[...].astype(F32) + dq2[...].astype(F32) + dq3[...].astype(F32)
    dkv = dkv0[...] + dkv1[...].astype(F32) + dkv2[...].astype(F32) + dkv3[...].astype(F32)
    dq, dkv = dq.astype(BF16), dkv.astype(BF16)
    for j in range(RUNS):
        zh, c = divmod(j, 2)
        one_hot = placing(copy_ref, j).T.astype(BF16)
        at = 64 * c
        queries = jnp.concatenate(
            [dq[256 * zh + at : 256 * zh + at + 64], dq[256 * zh + 128 + at : 256 * zh + 192 + at]], axis=0
        )
        keys = jnp.concatenate(
            [dkvn_ref[128 * zh + at : 128 * zh + at + 64, :], dkv[128 * zh + at : 128 * zh + at + 64]], axis=0
        )
        moved = contract(one_hot, jnp.concatenate([queries, keys], axis=1), 1, 0).astype(BF16)
        for z in range(4):
            for i in range(3):
                out_ref[4 * j + z, 32 * i : 32 * i + 32, :] = moved[32 * z : 32 * z + 32, HD * i : HD * (i + 1)]


def unpack_kernel(got_ref, dq_ref, dk_ref, dv_ref):
    rows = dq_ref.shape[0]
    for slot in range(16):
        j, z = divmod(slot, 4)
        h = 4 * z + j
        for i, ref in enumerate((dq_ref, dk_ref, dv_ref)):
            ref[:, h * HD : (h + 1) * HD] = got_ref[slot, i * rows : (i + 1) * rows, :]


def swap(x, axes, mask):
    return lax.ppermute(x, axes, [(i, i ^ mask) for i in range(4)])


def shape(dims, dtype=BF16):
    return jax.ShapeDtypeStruct(dims, dtype)


def per_device(query_in, key_in, value_in, saved_out, grad_out, saved_lse, row_block, row_copy):
    copies = row_copy.reshape(-1, RUN)
    ids = row_block[:: 4 * RUN]
    rows = query_in.shape[0]
    packed = call(
        pack_kernel,
        shape((16, 4 * rows + 16, HD)),
        (query_in, key_in, value_in, saved_out, grad_out, saved_lse.T),
    )
    got = lax.all_to_all(packed, HEAD_AXES, 0, 0, tiled=True)
    qd, kv, kvn = call(
        sort_kernel, (shape((528, 256)), shape((256, 256)), shape((256, 256))), (got, copies)
    )
    qds = [qd] + [None] * 3
    kvs = [kv] + [None] * 3
    for m in (2, 1, 3):
        qds[m] = swap(qd, QUERY_AXES, m)
        kvs[m] = swap(kv, KEY_AXES, m)
    outs = (
        [shape((512, HD), F32)] + [shape((512, HD))] * 3
        + [shape((256, 256), F32)] + [shape((256, 256))] * 3 + [shape((256, 256))]
    )
    scratch = (
        pltpu.VMEM((4, 512, HD), BF16), pltpu.VMEM((4, 512, HD), BF16),
        pltpu.VMEM((4, 1, 512), F32), pltpu.VMEM((4, 1, 512), F32),
        pltpu.VMEM((8, 128, HD), BF16), pltpu.VMEM((8, HD, 128), BF16), pltpu.VMEM((8, 128, HD), BF16),
        pltpu.VMEM((4, HD, 512), F32), pltpu.VMEM((8, 128, HD), F32), pltpu.VMEM((8, 128, HD), F32),
    )
    results = call(attend_kernel, outs, (ids, *qds, *kvs, kvn), smem=(0,), scratch=scratch)
    dqs, dkvs, dkvn = list(results[:4]), list(results[4:8]), results[8]
    for m in (2, 1, 3):
        dqs[m] = swap(dqs[m], QUERY_AXES, m)
        dkvs[m] = swap(dkvs[m], KEY_AXES, m)
    back = call(unsort_kernel, shape((16, 3 * rows, HD)), (*dqs, *dkvs, dkvn, copies))
    back = lax.all_to_all(back, HEAD_AXES, 0, 0, tiled=True)
    return call(unpack_kernel, (shape((rows, 16 * HD)),) * 3, (back,))


def solution(mesh):
    fine = Mesh(mesh.devices.reshape(SIZES), AXES)
    whole = P(AXES, None)
    return jax.shard_map(
        per_device,
        mesh=fine,
        in_specs=(whole, whole, whole, whole, whole, P(AXES[:5], AXES[5]), P(), P()),
        out_specs=(whole, whole, whole),
        check_vma=False,
    )
```

```python
import jax
import jax.numpy as jnp
from jax import lax
from jax.experimental import pallas as pl
from jax.experimental.pallas import tpu as pltpu
from jax.sharding import Mesh
from jax.sharding import PartitionSpec as P

HD = 128
RUN = 128
HALF = RUN // 2
AXES = ("y", "zh", "xh", "xl", "c", "zl")
SIZES = (4, 2, 2, 2, 2, 4)
HEAD_AXES = ("zl", "zh", "xl")
QUERY_AXES = ("xh", "c")
RUNS = 4
SCALE = HD**-0.5
LOG2E = 1.4426950408889634
F32 = jnp.float32
BF16 = jnp.bfloat16
VMEM = pl.BlockSpec(memory_space=pltpu.VMEM)
HBM = pl.BlockSpec(memory_space=pltpu.HBM)
SMEM = pl.BlockSpec(memory_space=pltpu.SMEM)


def iota(shape, axis):
    return lax.broadcasted_iota(jnp.int32, shape, axis)


def split_two(x):
    high = x.astype(BF16).astype(F32)
    return high, x - high


def contract(a, b, dim_a, dim_b):
    return lax.dot_general(a, b, (((dim_a,), (dim_b,)), ((), ())), preferred_element_type=F32)


def call(body, out_shape, args, smem=(), hbm=(), scratch=(), limit=32 << 20, cost=None):
    return pl.pallas_call(
        body,
        out_shape=out_shape,
        in_specs=[SMEM if i in smem else HBM if i in hbm else VMEM for i in range(len(args))],
        out_specs=jax.tree.map(lambda _: VMEM, out_shape),
        scratch_shapes=list(scratch),
        compiler_params=pltpu.CompilerParams(vmem_limit_bytes=limit),
        cost_estimate=cost,
    )(*args)


def pack_kernel(q_in, k_in, v_in, o_in, g_in, lse_in, out_ref, q_ref, k_ref, v_ref, o_ref, g_ref, lse_ref, sems):
    pairs = ((g_in, g_ref), (o_in, o_ref), (lse_in, lse_ref), (q_in, q_ref), (k_in, k_ref), (v_in, v_ref))
    copies = [pltpu.make_async_copy(a, b, sems.at[i]) for i, (a, b) in enumerate(pairs)]
    for copy in copies:
        copy.start()
    rows = q_ref.shape[0]
    for copy in copies[:3]:
        copy.wait()
    lane = iota((rows, 128), 1)
    delta = jnp.zeros((rows, 128), F32)
    for h in range(16):
        cols = slice(h * HD, (h + 1) * HD)
        term = g_ref[:, cols].astype(F32) * o_ref[:, cols].astype(F32)
        delta = jnp.where(lane == h, jnp.sum(term, axis=1, keepdims=True), delta)
    delta = jnp.concatenate([delta, jnp.zeros((128 - rows, 128), F32)], axis=0).T
    delta_high, delta_low = split_two(delta)
    lse_high, lse_low = split_two(lse_ref[...])
    row = iota((16, 128), 0)
    for copy in copies[3:]:
        copy.wait()
    for h in range(16):
        j = h % 4
        cols = slice(h * HD, (h + 1) * HD)
        for i, ref in enumerate((q_ref, g_ref, k_ref, v_ref)):
            out_ref[h, i * rows : (i + 1) * rows, :] = ref[:, cols]
        stats = jnp.where(row == 0, lse_high[j : j + 1], 0.0)
        stats = jnp.where(row == 1, lse_low[j : j + 1], stats)
        stats = jnp.where(row == 2, delta_high[h : h + 1], stats)
        stats = jnp.where(row == 3, delta_low[h : h + 1], stats)
        out_ref[h, 4 * rows : 4 * rows + 16, :] = stats.astype(BF16)


def placing(copy_ref, j):
    zh, xl = divmod(j, 2)
    shard = ((lax.axis_index("y") * 2 + zh) * 4 + lax.axis_index("xh") * 2 + xl) * 2 + lax.axis_index("c")
    copy = jnp.broadcast_to(copy_ref[pl.ds(shard, 1), :], (8, RUN)).astype(F32)
    upto = (iota((RUN, RUN), 0) <= iota((RUN, RUN), 1)).astype(BF16)
    count = contract(copy.astype(BF16), upto, 1, 0)
    index = iota((8, RUN), 1).astype(F32)
    place = jnp.where(copy > 0.5, HALF - 1.0 + count, index - count)
    place = jnp.broadcast_to(place[0:1], (RUN, RUN)).astype(jnp.int32)
    return (iota((RUN, RUN), 0) == place).astype(F32)


def sort_kernel(got_ref, copy_ref, qd_ref, kv_ref, kvn_ref):
    zl = lax.axis_index("zl")
    row = iota((16, RUN), 0)
    stats = []
    for j in range(RUNS):
        zh, xl = divmod(j, 2)
        one_hot = placing(copy_ref, j).astype(BF16)
        parts = [
            jnp.concatenate([got_ref[4 * z + j, 32 * i : 32 * i + 32, :] for z in range(4)], axis=0)
            for i in range(4)
        ]
        moved = contract(one_hot, jnp.concatenate(parts, axis=1), 1, 0).astype(BF16)
        qd_ref[256 * zh + 64 * xl : 256 * zh + 64 * xl + 64, :] = moved[:HALF, :256]
        qd_ref[256 * zh + 128 + 64 * xl : 256 * zh + 192 + 64 * xl, :] = moved[HALF:, :256]
        kvn_ref[128 * zh + 64 * xl : 128 * zh + 64 * xl + 64, :] = moved[:HALF, 256:]
        for y in range(4):
            kv_ref[y, 128 * zh + 64 * xl : 128 * zh + 64 * xl + 64, :] = moved[HALF:, 256:]
        lse = got_ref[4 * zl + j, 128:144, :].astype(F32)
        delta = jnp.concatenate(
            [got_ref[4 * z + j, 128:144, :].astype(F32)[:, :32] for z in range(4)], axis=1
        )
        both = jnp.where(row < 2, lse, delta).astype(BF16)
        stats.append(contract(both, one_hot, 1, 1))
    halves = []
    for zh in range(2):
        a, b = stats[2 * zh], stats[2 * zh + 1]
        halves.append(
            jnp.concatenate([a[:8, :HALF], b[:8, :HALF], a[:8, HALF:], b[:8, HALF:]], axis=1)
        )
    qd_ref[512:528, :] = jnp.concatenate(halves, axis=0).astype(BF16)


def tile(k, kt, v, q, g, lse, delta):
    scores = contract(k, q, 1, 1)
    weights = jnp.exp2(scores * (SCALE * LOG2E) - lse)
    dweights = contract(v, g, 1, 1)
    dscores = (weights * (dweights - delta)).astype(BF16)
    dv = contract(weights.astype(BF16), g, 1, 0)
    dk = contract(dscores, q, 1, 0)
    dq = contract(kt, dscores, 1, 0)
    return dv, dk, dq


def attend_kernel(
    ids_ref, qd0, qd1, qd2, qd3, kv_ref, kvn_ref,
    dq_keep, dq_send, dkv_ref, dkvn_ref,
    q_all, g_all, lse_all, delta_all, k_all, kt_all, v_all, dqt, dk_all, dv_all,
):
    y, xh = lax.axis_index("y"), lax.axis_index("xh")
    for m, ref in enumerate((qd0, qd1, qd2, qd3)):
        stats = ref[512:528, :].astype(F32)
        for zh in range(2):
            block, at = zh * 2 + m // 2, 256 * (m % 2)
            q_all[block, at : at + 256, :] = ref[256 * zh : 256 * zh + 256, :HD]
            g_all[block, at : at + 256, :] = ref[256 * zh : 256 * zh + 256, HD:]
            s = 8 * zh
            lse_all[block, :, at : at + 256] = (stats[s : s + 1] + stats[s + 1 : s + 2]) * LOG2E
            delta_all[block, :, at : at + 256] = stats[s + 2 : s + 3] + stats[s + 3 : s + 4]
    for d in range(4):
        for zh in range(2):
            n = 2 * d + zh
            k = kv_ref[d, 128 * zh : 128 * zh + 128, :HD]
            k_all[n] = k
            kt_all[n] = k.astype(F32).T.astype(BF16)
            v_all[n] = kv_ref[d, 128 * zh : 128 * zh + 128, HD:]
    dk_all[...] = jnp.zeros_like(dk_all)
    dv_all[...] = jnp.zeros_like(dv_all)

    for zh in range(2):
        block, n = zh * 2, 2 * y + zh
        kn = kvn_ref[128 * zh : 128 * zh + 128, :HD]
        vn = kvn_ref[128 * zh : 128 * zh + 128, HD:]
        knt = kn.astype(F32).T.astype(BF16)
        for copy in range(2):
            first, second = 128 * copy, 256 + 128 * copy

            def rows(ref):
                return jnp.concatenate([ref[block, first : first + 128, :], ref[block, second : second + 128, :]], axis=0)

            def lanes(ref):
                return jnp.concatenate([ref[block, :, first : first + 128], ref[block, :, second : second + 128]], axis=1)

            q, g, lse, delta = rows(q_all), rows(g_all), lanes(lse_all), lanes(delta_all)
            if copy == 0:
                dv, dk, dq = tile(kn, knt, vn, q, g, lse, delta)
                dkvn_ref[128 * zh : 128 * zh + 128, :] = jnp.concatenate([dk * SCALE, dv], axis=1).astype(BF16)
            else:
                dv, dk, dq = tile(k_all[n], kt_all[n], v_all[n], q, g, lse, delta)
                dk_all[n] = dk
                dv_all[n] = dv
            dqt[block, :, first : first + 128] = dq[:, :128]
            dqt[block, :, second : second + 128] = dq[:, 128:]
    for zh in range(2):
        dqt[zh * 2 + 1] = jnp.zeros((HD, 512), F32)

    for block in range(4):
        zq, other = divmod(block, 2)
        own_id = ids_ref[(y * 2 + zq) * 2 + (xh ^ other)]

        def step(n, carry, block=block, own_id=own_id):
            key_id = ids_ref[2 * n + xh]

            @pl.when(key_id < own_id)
            def _():
                dv, dk, dq = tile(
                    k_all[n], kt_all[n], v_all[n], q_all[block], g_all[block], lse_all[block], delta_all[block]
                )
                dv_all[n] += dv
                dk_all[n] += dk
                dqt[block] += dq

            return carry

        lax.fori_loop(0, 8, step, 0)

    for m in range(4):
        ref = dq_send if m % 2 else dq_keep
        for zh in range(2):
            block, at = zh * 2 + m // 2, 256 * (m % 2)
            ref[m // 2, 256 * zh : 256 * zh + 256, :] = (dqt[block, :, at : at + 256].T * SCALE).astype(ref.dtype)
    for d in range(4):
        for zh in range(2):
            n = 2 * d + zh
            dkv_ref[d, 128 * zh : 128 * zh + 128, :HD] = (dk_all[n] * SCALE).astype(BF16)
            dkv_ref[d, 128 * zh : 128 * zh + 128, HD:] = dv_all[n].astype(BF16)


def add_kernel(keep_ref, got_ref, out_ref):
    out_ref[...] = (keep_ref[1] + got_ref[1].astype(F32)).astype(BF16)


def unsort_kernel(keep_ref, got_core, got_chip, got_dkv, dkvn_ref, copy_ref, out_ref):
    dq = (keep_ref[0] + got_core[0].astype(F32) + got_chip[...].astype(F32)).astype(BF16)
    dkv = [got_dkv[y].astype(F32) for y in range(4)]
    dkv = (dkv[0] + dkv[1] + dkv[2] + dkv[3]).astype(BF16)
    for j in range(RUNS):
        zh, xl = divmod(j, 2)
        one_hot = placing(copy_ref, j).T.astype(BF16)
        at = 64 * xl
        queries = jnp.concatenate(
            [dq[256 * zh + at : 256 * zh + at + 64], dq[256 * zh + 128 + at : 256 * zh + 192 + at]], axis=0
        )
        keys = jnp.concatenate(
            [dkvn_ref[128 * zh + at : 128 * zh + at + 64, :], dkv[128 * zh + at : 128 * zh + at + 64]], axis=0
        )
        moved = contract(one_hot, jnp.concatenate([queries, keys], axis=1), 1, 0).astype(BF16)
        for z in range(4):
            for i in range(3):
                out_ref[4 * z + j, 32 * i : 32 * i + 32, :] = moved[32 * z : 32 * z + 32, HD * i : HD * (i + 1)]


def unpack_kernel(got_ref, dq_ref, dk_ref, dv_ref):
    rows = dq_ref.shape[0]
    for h in range(16):
        for i, ref in enumerate((dq_ref, dk_ref, dv_ref)):
            ref[:, h * HD : (h + 1) * HD] = got_ref[h, i * rows : (i + 1) * rows, :]


def swap(x, mask):
    return lax.ppermute(x, QUERY_AXES, [(i, i ^ mask) for i in range(4)])


def shape(dims, dtype=BF16):
    return jax.ShapeDtypeStruct(dims, dtype)


def per_device(query_in, key_in, value_in, saved_out, grad_out, saved_lse, row_block, row_copy):
    copies = row_copy.reshape(-1, RUN)
    ids = row_block[:: 4 * RUN]
    rows = query_in.shape[0]
    packed = call(
        pack_kernel,
        shape((16, 4 * rows + 16, HD)),
        (query_in, key_in, value_in, saved_out, grad_out, saved_lse.T),
        hbm=range(6),
        limit=62 << 20,
        scratch=[pltpu.VMEM(query_in.shape, BF16)] * 5 + [pltpu.VMEM((4, 128), F32), pltpu.SemaphoreType.DMA((6,))],
    )
    got = lax.all_to_all(packed, HEAD_AXES, 0, 0, tiled=True)
    qd, kv, kvn = call(
        sort_kernel, (shape((528, 256)), shape((4, 256, 256)), shape((256, 256))), (got, copies)
    )
    qd2 = swap(qd, 2)
    kvs = lax.all_to_all(kv, "y", 0, 0, tiled=True)
    qd1 = swap(qd, 1)
    qd3 = swap(qd2, 1)
    outs = (shape((2, 512, HD), F32), shape((2, 512, HD)), shape((4, 256, 256)), shape((256, 256)))
    scratch = (
        pltpu.VMEM((4, 512, HD), BF16), pltpu.VMEM((4, 512, HD), BF16),
        pltpu.VMEM((4, 1, 512), F32), pltpu.VMEM((4, 1, 512), F32),
        pltpu.VMEM((8, 128, HD), BF16), pltpu.VMEM((8, HD, 128), BF16), pltpu.VMEM((8, 128, HD), BF16),
        pltpu.VMEM((4, HD, 512), F32), pltpu.VMEM((8, 128, HD), F32), pltpu.VMEM((8, 128, HD), F32),
    )
    dq_keep, dq_send, dkv, dkvn = call(
        attend_kernel, outs, (ids, qd, qd1, qd2, qd3, kvs, kvn), smem=(0,), scratch=scratch
    )
    dq_core = swap(dq_send, 1)
    dkvs = lax.all_to_all(dkv, "y", 0, 0, tiled=True)
    dq_chip = swap(call(add_kernel, shape((512, HD)), (dq_keep, dq_core)), 2)
    back = call(unsort_kernel, shape((16, 3 * rows, HD)), (dq_keep, dq_core, dq_chip, dkvs, dkvn, copies))
    back = lax.all_to_all(back, HEAD_AXES, 0, 0, tiled=True)
    return call(unpack_kernel, (shape((rows, 16 * HD)),) * 3, (back,))


def solution(mesh):
    fine = Mesh(mesh.devices.reshape(SIZES), AXES)
    whole = P(AXES, None)
    return jax.shard_map(
        per_device,
        mesh=fine,
        in_specs=(whole, whole, whole, whole, whole, P(AXES[:5], AXES[5]), P(), P()),
        out_specs=(whole, whole, whole),
        check_vma=False,
    )
```

```python
import jax
import jax.numpy as jnp
from jax import lax
from jax.experimental import pallas as pl
from jax.experimental.pallas import tpu as pltpu
from jax.sharding import Mesh
from jax.sharding import PartitionSpec as P

HD = 128
RUN = 128
HALF = RUN // 2
AXES = ("y", "zh", "xh", "xl", "c", "zl")
SIZES = (4, 2, 2, 2, 2, 4)
HEAD_AXES = ("zl", "zh", "xl")
QUERY_AXES = ("xh", "c")
RUNS = 4
SCALE = HD**-0.5
LOG2E = 1.4426950408889634
OFF = 1e30
F32 = jnp.float32
BF16 = jnp.bfloat16
VMEM = pl.BlockSpec(memory_space=pltpu.VMEM)
HBM = pl.BlockSpec(memory_space=pltpu.HBM)
SMEM = pl.BlockSpec(memory_space=pltpu.SMEM)


def iota(shape, axis):
    return lax.broadcasted_iota(jnp.int32, shape, axis)


def split_two(x):
    high = x.astype(BF16).astype(F32)
    return high, x - high


def contract(a, b, dim_a, dim_b):
    return lax.dot_general(a, b, (((dim_a,), (dim_b,)), ((), ())), preferred_element_type=F32)


def call(body, out_shape, args, smem=(), hbm=(), scratch=(), limit=32 << 20, cost=None):
    return pl.pallas_call(
        body,
        out_shape=out_shape,
        in_specs=[SMEM if i in smem else HBM if i in hbm else VMEM for i in range(len(args))],
        out_specs=jax.tree.map(lambda _: VMEM, out_shape),
        scratch_shapes=list(scratch),
        compiler_params=pltpu.CompilerParams(vmem_limit_bytes=limit),
        cost_estimate=cost,
    )(*args)


def pack_kernel(q_in, k_in, v_in, o_in, g_in, lse_in, out_ref, q_ref, k_ref, v_ref, o_ref, g_ref, lse_ref, sems):
    pairs = ((g_in, g_ref), (o_in, o_ref), (lse_in, lse_ref), (q_in, q_ref), (k_in, k_ref), (v_in, v_ref))
    copies = [pltpu.make_async_copy(a, b, sems.at[i]) for i, (a, b) in enumerate(pairs)]
    for copy in copies:
        copy.start()
    rows = q_ref.shape[0]
    for copy in copies[:3]:
        copy.wait()
    lane = iota((rows, 128), 1)
    delta = jnp.zeros((rows, 128), F32)
    for h in range(16):
        cols = slice(h * HD, (h + 1) * HD)
        term = g_ref[:, cols].astype(F32) * o_ref[:, cols].astype(F32)
        delta = jnp.where(lane == h, jnp.sum(term, axis=1, keepdims=True), delta)
    delta = jnp.concatenate([delta, jnp.zeros((128 - rows, 128), F32)], axis=0).T
    delta_high, delta_low = split_two(delta)
    lse_high, lse_low = split_two(lse_ref[...])
    row = iota((16, 128), 0)
    for copy in copies[3:]:
        copy.wait()
    for h in range(16):
        j = h % 4
        cols = slice(h * HD, (h + 1) * HD)
        for i, ref in enumerate((q_ref, g_ref, k_ref, v_ref)):
            out_ref[h, i * rows : (i + 1) * rows, :] = ref[:, cols]
        stats = jnp.where(row == 0, lse_high[j : j + 1], 0.0)
        stats = jnp.where(row == 1, lse_low[j : j + 1], stats)
        stats = jnp.where(row == 2, delta_high[h : h + 1], stats)
        stats = jnp.where(row == 3, delta_low[h : h + 1], stats)
        out_ref[h, 4 * rows : 4 * rows + 16, :] = stats.astype(BF16)


def placing(copy_ref, j):
    zh, xl = divmod(j, 2)
    shard = ((lax.axis_index("y") * 2 + zh) * 4 + lax.axis_index("xh") * 2 + xl) * 2 + lax.axis_index("c")
    copy = jnp.broadcast_to(copy_ref[pl.ds(shard, 1), :], (8, RUN)).astype(F32)
    upto = (iota((RUN, RUN), 0) <= iota((RUN, RUN), 1)).astype(BF16)
    count = contract(copy.astype(BF16), upto, 1, 0)
    index = iota((8, RUN), 1).astype(F32)
    place = jnp.where(copy > 0.5, HALF - 1.0 + count, index - count)
    place = jnp.broadcast_to(place[0:1], (RUN, RUN)).astype(jnp.int32)
    return (iota((RUN, RUN), 0) == place).astype(F32)


def sort_kernel(got_ref, copy_ref, qd_ref, kv_ref, kvn_ref):
    zl = lax.axis_index("zl")
    row = iota((16, RUN), 0)
    stats = []
    for j in range(RUNS):
        zh, xl = divmod(j, 2)
        one_hot = placing(copy_ref, j).astype(BF16)
        parts = [
            jnp.concatenate([got_ref[4 * z + j, 32 * i : 32 * i + 32, :] for z in range(4)], axis=0)
            for i in range(4)
        ]
        moved = contract(one_hot, jnp.concatenate(parts, axis=1), 1, 0).astype(BF16)
        qd_ref[256 * zh + 64 * xl : 256 * zh + 64 * xl + 64, :] = moved[:HALF, :256]
        qd_ref[256 * zh + 128 + 64 * xl : 256 * zh + 192 + 64 * xl, :] = moved[HALF:, :256]
        kvn_ref[128 * zh + 64 * xl : 128 * zh + 64 * xl + 64, :] = moved[:HALF, 256:]
        for y in range(4):
            kv_ref[y, 128 * zh + 64 * xl : 128 * zh + 64 * xl + 64, :] = moved[HALF:, 256:]
        lse = got_ref[4 * zl + j, 128:144, :].astype(F32)
        delta = jnp.concatenate(
            [got_ref[4 * z + j, 128:144, :].astype(F32)[:, :32] for z in range(4)], axis=1
        )
        both = jnp.where(row < 2, lse, delta).astype(BF16)
        stats.append(contract(both, one_hot, 1, 1))
    halves = []
    for zh in range(2):
        a, b = stats[2 * zh], stats[2 * zh + 1]
        halves.append(
            jnp.concatenate([a[:8, :HALF], b[:8, :HALF], a[:8, HALF:], b[:8, HALF:]], axis=1)
        )
    qd_ref[512:528, :] = jnp.concatenate(halves, axis=0).astype(BF16)


def attend_kernel(
    ids_ref, qd0, qd1, qd2, qd3, kv_ref, kvn_ref,
    dq_keep, dq_send, dkv_ref, dkvn_ref,
    q_all, g_all, lse_all, delta_all, k_all, kt_all, v_all, dk_all, dv_all,
):
    y, xh = lax.axis_index("y"), lax.axis_index("xh")
    for m, ref in enumerate((qd0, qd1, qd2, qd3)):
        stats = ref[512:528, :].astype(F32)
        for zh in range(2):
            block, at = zh * 2 + m // 2, 256 * (m % 2)
            q_all[block, at : at + 256, :] = ref[256 * zh : 256 * zh + 256, :HD]
            g_all[block, at : at + 256, :] = ref[256 * zh : 256 * zh + 256, HD:]
            s = 8 * zh
            lse_all[block, :, at : at + 256] = (stats[s : s + 1] + stats[s + 1 : s + 2]) * LOG2E
            delta_all[block, :, at : at + 256] = stats[s + 2 : s + 3] + stats[s + 3 : s + 4]
    for first, ref in ((0, kvn_ref.at[:128]), (1152, kvn_ref.at[128:])) + tuple(
        (128 + 256 * d, kv_ref.at[d]) for d in range(4)
    ):
        size = ref.shape[0]
        k = ref[:, :HD]
        k_all[first : first + size, :] = k
        v_all[first : first + size, :] = ref[:, HD:]
        kt_all[:, first : first + size] = k.astype(F32).T.astype(BF16)

    clean = iota((1, 512), 1) // 128 % 2 == 1
    for block in (1, 3, 0, 2):
        zh, other = divmod(block, 2)
        own_id = ids_ref[(y * 2 + zh) * 2 + (xh ^ other)]
        lse, delta = lse_all[block], delta_all[block]
        limits = []
        for n in range(8):
            key_id = ids_ref[2 * n + xh]
            noisy_off = jnp.where(key_id < own_id, 0.0, OFF)
            clean_off = jnp.where(key_id <= own_id, 0.0, OFF)
            limits.append(lse + jnp.where(clean, clean_off, noisy_off))
        first, last = 128, 1152
        if not other:
            own_noisy = lse + jnp.where(clean, OFF, 0.0)
            limits = limits + [own_noisy] if zh else [own_noisy] + limits
            first, last = (128, 1280) if zh else (0, 1152)
        q, g = q_all[block], g_all[block]
        scores = contract(k_all[first:last, :], q, 1, 1)
        weights = jnp.concatenate(
            [jnp.exp2(scores[128 * i : 128 * i + 128] * (SCALE * LOG2E) - row) for i, row in enumerate(limits)],
            axis=0,
        )
        dweights = contract(v_all[first:last, :], g, 1, 1)
        dscores = (weights * (dweights - delta)).astype(BF16)
        dv = contract(weights.astype(BF16), g, 1, 0)
        dk = contract(dscores, q, 1, 0)
        if block == 1:
            dk_all[first:last, :] = dk
            dv_all[first:last, :] = dv
            zeros = jnp.zeros((128, HD), F32)
            for ref in (dk_all, dv_all):
                ref[:128, :] = zeros
                ref[1152:, :] = zeros
        else:
            dk_all[first:last, :] += dk
            dv_all[first:last, :] += dv
        dq = contract(kt_all[:, first:last], dscores, 1, 0).T * SCALE
        dq_keep[other, 256 * zh : 256 * zh + 256, :] = dq[:256]
        dq_send[other, 256 * zh : 256 * zh + 256, :] = dq[256:].astype(BF16)
    for first, ref in ((0, dkvn_ref.at[:128]), (1152, dkvn_ref.at[128:])) + tuple(
        (128 + 256 * d, dkv_ref.at[d]) for d in range(4)
    ):
        size = ref.shape[0]
        ref[:, :HD] = (dk_all[first : first + size, :] * SCALE).astype(BF16)
        ref[:, HD:] = dv_all[first : first + size, :].astype(BF16)


def add_kernel(keep_ref, got_ref, out_ref):
    out_ref[...] = (keep_ref[1] + got_ref[1].astype(F32)).astype(BF16)


def unsort_kernel(keep_ref, got_core, got_chip, got_dkv, dkvn_ref, copy_ref, out_ref):
    dq = (keep_ref[0] + got_core[0].astype(F32) + got_chip[...].astype(F32)).astype(BF16)
    dkv = [got_dkv[y].astype(F32) for y in range(4)]
    dkv = (dkv[0] + dkv[1] + dkv[2] + dkv[3]).astype(BF16)
    for j in range(RUNS):
        zh, xl = divmod(j, 2)
        one_hot = placing(copy_ref, j).T.astype(BF16)
        at = 64 * xl
        queries = jnp.concatenate(
            [dq[256 * zh + at : 256 * zh + at + 64], dq[256 * zh + 128 + at : 256 * zh + 192 + at]], axis=0
        )
        keys = jnp.concatenate(
            [dkvn_ref[128 * zh + at : 128 * zh + at + 64, :], dkv[128 * zh + at : 128 * zh + at + 64]], axis=0
        )
        moved = contract(one_hot, jnp.concatenate([queries, keys], axis=1), 1, 0).astype(BF16)
        for z in range(4):
            for i in range(3):
                out_ref[4 * z + j, 32 * i : 32 * i + 32, :] = moved[32 * z : 32 * z + 32, HD * i : HD * (i + 1)]


def unpack_kernel(got_ref, dq_ref, dk_ref, dv_ref):
    rows = dq_ref.shape[0]
    for h in range(16):
        for i, ref in enumerate((dq_ref, dk_ref, dv_ref)):
            ref[:, h * HD : (h + 1) * HD] = got_ref[h, i * rows : (i + 1) * rows, :]


def swap(x, mask):
    return lax.ppermute(x, QUERY_AXES, [(i, i ^ mask) for i in range(4)])


def shape(dims, dtype=BF16):
    return jax.ShapeDtypeStruct(dims, dtype)


def per_device(query_in, key_in, value_in, saved_out, grad_out, saved_lse, row_block, row_copy):
    copies = row_copy.reshape(-1, RUN)
    ids = row_block[:: 4 * RUN]
    rows = query_in.shape[0]
    packed = call(
        pack_kernel,
        shape((16, 4 * rows + 16, HD)),
        (query_in, key_in, value_in, saved_out, grad_out, saved_lse.T),
        hbm=range(6),
        limit=62 << 20,
        scratch=[pltpu.VMEM(query_in.shape, BF16)] * 5 + [pltpu.VMEM((4, 128), F32), pltpu.SemaphoreType.DMA((6,))],
    )
    got = lax.all_to_all(packed, HEAD_AXES, 0, 0, tiled=True)
    qd, kv, kvn = call(
        sort_kernel, (shape((528, 256)), shape((4, 256, 256)), shape((256, 256))), (got, copies)
    )
    qd2 = swap(qd, 2)
    kvs = lax.all_to_all(kv, "y", 0, 0, tiled=True)
    qd1 = swap(qd, 1)
    qd3 = swap(qd2, 1)
    outs = (shape((2, 512, HD), F32), shape((2, 512, HD)), shape((4, 256, 256)), shape((256, 256)))
    scratch = (
        pltpu.VMEM((4, 512, HD), BF16), pltpu.VMEM((4, 512, HD), BF16),
        pltpu.VMEM((4, 1, 512), F32), pltpu.VMEM((4, 1, 512), F32),
        pltpu.VMEM((1280, HD), BF16), pltpu.VMEM((HD, 1280), BF16), pltpu.VMEM((1280, HD), BF16),
        pltpu.VMEM((1280, HD), F32), pltpu.VMEM((1280, HD), F32),
    )
    dq_keep, dq_send, dkv, dkvn = call(
        attend_kernel, outs, (ids, qd, qd1, qd2, qd3, kvs, kvn), smem=(0,), scratch=scratch
    )
    dq_core = swap(dq_send, 1)
    dkvs = lax.all_to_all(dkv, "y", 0, 0, tiled=True)
    dq_chip = swap(call(add_kernel, shape((512, HD)), (dq_keep, dq_core)), 2)
    back = call(unsort_kernel, shape((16, 3 * rows, HD)), (dq_keep, dq_core, dq_chip, dkvs, dkvn, copies))
    back = lax.all_to_all(back, HEAD_AXES, 0, 0, tiled=True)
    return call(unpack_kernel, (shape((rows, 16 * HD)),) * 3, (back,))


def solution(mesh):
    fine = Mesh(mesh.devices.reshape(SIZES), AXES)
    whole = P(AXES, None)
    return jax.shard_map(
        per_device,
        mesh=fine,
        in_specs=(whole, whole, whole, whole, whole, P(AXES[:5], AXES[5]), P(), P()),
        out_specs=(whole, whole, whole),
        check_vma=False,
    )
```

```python
import jax
import jax.numpy as jnp
from jax import lax
from jax.experimental import pallas as pl
from jax.experimental.pallas import tpu as pltpu
from jax.sharding import Mesh
from jax.sharding import PartitionSpec as P

HD = 128
RUN = 128
HALF = RUN // 2
AXES = ("y", "zh", "xh", "xl", "c", "zl")
SIZES = (4, 2, 2, 2, 2, 4)
HEAD_AXES = ("zl", "zh", "xl")
QUERY_AXES = ("xh", "c")
RUNS = 4
SCALE = HD**-0.5
LOG2E = 1.4426950408889634
OFF = 1e30
F32 = jnp.float32
BF16 = jnp.bfloat16
VMEM = pl.BlockSpec(memory_space=pltpu.VMEM)
HBM = pl.BlockSpec(memory_space=pltpu.HBM)
SMEM = pl.BlockSpec(memory_space=pltpu.SMEM)


def iota(shape, axis):
    return lax.broadcasted_iota(jnp.int32, shape, axis)


def split_two(x):
    high = x.astype(BF16).astype(F32)
    return high, x - high


def contract(a, b, dim_a, dim_b):
    return lax.dot_general(a, b, (((dim_a,), (dim_b,)), ((), ())), preferred_element_type=F32)


def call(body, out_shape, args, smem=(), hbm=(), scratch=(), limit=32 << 20, cost=None):
    return pl.pallas_call(
        body,
        out_shape=out_shape,
        in_specs=[SMEM if i in smem else HBM if i in hbm else VMEM for i in range(len(args))],
        out_specs=jax.tree.map(lambda _: VMEM, out_shape),
        scratch_shapes=list(scratch),
        compiler_params=pltpu.CompilerParams(vmem_limit_bytes=limit),
        cost_estimate=cost,
    )(*args)


def pack_kernel(q_in, k_in, v_in, o_in, g_in, lse_in, out_ref, q_ref, k_ref, v_ref, o_ref, g_ref, lse_ref, sems):
    pairs = ((g_in, g_ref), (o_in, o_ref), (lse_in, lse_ref), (q_in, q_ref), (k_in, k_ref), (v_in, v_ref))
    copies = [pltpu.make_async_copy(a, b, sems.at[i]) for i, (a, b) in enumerate(pairs)]
    for copy in copies:
        copy.start()
    rows = q_ref.shape[0]
    for copy in copies[:3]:
        copy.wait()
    lane = iota((rows, 128), 1)
    delta = jnp.zeros((rows, 128), F32)
    for h in range(16):
        cols = slice(h * HD, (h + 1) * HD)
        term = g_ref[:, cols].astype(F32) * o_ref[:, cols].astype(F32)
        delta = jnp.where(lane == h, jnp.sum(term, axis=1, keepdims=True), delta)
    delta = jnp.concatenate([delta, jnp.zeros((128 - rows, 128), F32)], axis=0).T
    delta_high, delta_low = split_two(delta)
    lse_high, lse_low = split_two(lse_ref[...])
    row = iota((16, 128), 0)
    for copy in copies[3:]:
        copy.wait()
    for h in range(16):
        j = h % 4
        cols = slice(h * HD, (h + 1) * HD)
        for i, ref in enumerate((q_ref, g_ref, k_ref, v_ref)):
            out_ref[h, i * rows : (i + 1) * rows, :] = ref[:, cols]
        stats = jnp.where(row == 0, lse_high[j : j + 1], 0.0)
        stats = jnp.where(row == 1, lse_low[j : j + 1], stats)
        stats = jnp.where(row == 2, delta_high[h : h + 1], stats)
        stats = jnp.where(row == 3, delta_low[h : h + 1], stats)
        out_ref[h, 4 * rows : 4 * rows + 16, :] = stats.astype(BF16)


def placing(copy_ref, j):
    zh, xl = divmod(j, 2)
    shard = ((lax.axis_index("y") * 2 + zh) * 4 + lax.axis_index("xh") * 2 + xl) * 2 + lax.axis_index("c")
    copy = jnp.broadcast_to(copy_ref[pl.ds(shard, 1), :], (8, RUN)).astype(F32)
    upto = (iota((RUN, RUN), 0) <= iota((RUN, RUN), 1)).astype(BF16)
    count = contract(copy.astype(BF16), upto, 1, 0)
    index = iota((8, RUN), 1).astype(F32)
    place = jnp.where(copy > 0.5, HALF - 1.0 + count, index - count)
    place = jnp.broadcast_to(place[0:1], (RUN, RUN)).astype(jnp.int32)
    return (iota((RUN, RUN), 0) == place).astype(F32)


def sort_kernel(got_ref, copy_ref, qd_ref, kv_ref, kvn_ref):
    zl = lax.axis_index("zl")
    row = iota((16, RUN), 0)
    stats = []
    for j in range(RUNS):
        zh, xl = divmod(j, 2)
        one_hot = placing(copy_ref, j).astype(BF16)
        parts = [
            jnp.concatenate([got_ref[4 * z + j, 32 * i : 32 * i + 32, :] for z in range(4)], axis=0)
            for i in range(4)
        ]
        moved = contract(one_hot, jnp.concatenate(parts, axis=1), 1, 0).astype(BF16)
        qd_ref[256 * zh + 64 * xl : 256 * zh + 64 * xl + 64, :] = moved[:HALF, :256]
        qd_ref[256 * zh + 128 + 64 * xl : 256 * zh + 192 + 64 * xl, :] = moved[HALF:, :256]
        kvn_ref[128 * zh + 64 * xl : 128 * zh + 64 * xl + 64, :] = moved[:HALF, 256:]
        for y in range(4):
            kv_ref[y, 128 * zh + 64 * xl : 128 * zh + 64 * xl + 64, :] = moved[HALF:, 256:]
        lse = got_ref[4 * zl + j, 128:144, :].astype(F32)
        delta = jnp.concatenate(
            [got_ref[4 * z + j, 128:144, :].astype(F32)[:, :32] for z in range(4)], axis=1
        )
        both = jnp.where(row < 2, lse, delta).astype(BF16)
        stats.append(contract(both, one_hot, 1, 1))
    halves = []
    for zh in range(2):
        a, b = stats[2 * zh], stats[2 * zh + 1]
        halves.append(
            jnp.concatenate([a[:8, :HALF], b[:8, :HALF], a[:8, HALF:], b[:8, HALF:]], axis=1)
        )
    qd_ref[512:528, :] = jnp.concatenate(halves, axis=0).astype(BF16)


def attend_kernel(
    ids_ref, qd0, qd1, qd2, qd3, kv_ref, kvn_ref,
    dq_keep, dq_send, dkv0, dkv1, dkv2, dkv3, dkvn_ref,
    q_all, g_all, lse_all, delta_all, k_all, kt_all, v_all, dk_all, dv_all,
):
    y, xh = lax.axis_index("y"), lax.axis_index("xh")
    for m, ref in enumerate((qd0, qd1, qd2, qd3)):
        stats = ref[512:528, :].astype(F32)
        for zh in range(2):
            block, at = zh * 2 + m // 2, 256 * (m % 2)
            q_all[block, at : at + 256, :] = ref[256 * zh : 256 * zh + 256, :HD]
            g_all[block, at : at + 256, :] = ref[256 * zh : 256 * zh + 256, HD:]
            s = 8 * zh
            lse_all[block, :, at : at + 256] = (stats[s : s + 1] + stats[s + 1 : s + 2]) * LOG2E
            delta_all[block, :, at : at + 256] = stats[s + 2 : s + 3] + stats[s + 3 : s + 4]
    for first, ref in ((0, kvn_ref.at[:128]), (1152, kvn_ref.at[128:])) + tuple(
        (128 + 256 * d, kv_ref.at[d]) for d in range(4)
    ):
        size = ref.shape[0]
        k = ref[:, :HD]
        k_all[first : first + size, :] = k
        v_all[first : first + size, :] = ref[:, HD:]
        kt_all[:, first : first + size] = k.astype(F32).T.astype(BF16)

    clean = iota((1, 512), 1) // 128 % 2 == 1
    for block in (1, 3, 0, 2):
        zh, other = divmod(block, 2)
        own_id = ids_ref[(y * 2 + zh) * 2 + (xh ^ other)]
        lse, delta = lse_all[block], delta_all[block]
        limits = []
        for n in range(8):
            key_id = ids_ref[2 * n + xh]
            noisy_off = jnp.where(key_id < own_id, 0.0, OFF)
            clean_off = jnp.where(key_id <= own_id, 0.0, OFF)
            limits.append(lse + jnp.where(clean, clean_off, noisy_off))
        first, last = 128, 1152
        if not other:
            own_noisy = lse + jnp.where(clean, OFF, 0.0)
            limits = limits + [own_noisy] if zh else [own_noisy] + limits
            first, last = (128, 1280) if zh else (0, 1152)
        q, g = q_all[block], g_all[block]
        scores = contract(k_all[first:last, :], q, 1, 1)
        weights = jnp.concatenate(
            [jnp.exp2(scores[128 * i : 128 * i + 128] * (SCALE * LOG2E) - row) for i, row in enumerate(limits)],
            axis=0,
        )
        dweights = contract(v_all[first:last, :], g, 1, 1)
        dscores = (weights * (dweights - delta)).astype(BF16)
        dv = contract(weights.astype(BF16), g, 1, 0)
        dk = contract(dscores, q, 1, 0)
        if block == 1:
            dk_all[first:last, :] = dk
            dv_all[first:last, :] = dv
            zeros = jnp.zeros((128, HD), F32)
            for ref in (dk_all, dv_all):
                ref[:128, :] = zeros
                ref[1152:, :] = zeros
        else:
            dk_all[first:last, :] += dk
            dv_all[first:last, :] += dv
        dq = contract(kt_all[:, first:last], dscores, 1, 0).T * SCALE
        dq_keep[other, 256 * zh : 256 * zh + 256, :] = dq[:256]
        dq_send[other, 256 * zh : 256 * zh + 256, :] = dq[256:].astype(BF16)
    pieces = [(0, dkvn_ref.at[:128]), (1152, dkvn_ref.at[128:])]
    for m, ref in enumerate((dkv0, dkv1, dkv2, dkv3)):
        pieces.append((pl.multiple_of(128 + 256 * (y ^ m), 128), ref))
    for first, ref in pieces:
        rows = pl.ds(first, ref.shape[0])
        ref[:, :HD] = (dk_all[rows, :] * SCALE).astype(ref.dtype)
        ref[:, HD:] = dv_all[rows, :].astype(ref.dtype)


def add_kernel(keep_ref, got_ref, out_ref):
    out_ref[...] = (keep_ref[1] + got_ref[1].astype(F32)).astype(BF16)


def unsort_kernel(keep_ref, got_core, got_chip, dkv0, dkv1, dkv2, dkv3, dkvn_ref, copy_ref, out_ref):
    dq = (keep_ref[0] + got_core[0].astype(F32) + got_chip[...].astype(F32)).astype(BF16)
    dkv = (dkv0[...] + dkv1[...].astype(F32) + dkv2[...].astype(F32) + dkv3[...].astype(F32)).astype(BF16)
    for j in range(RUNS):
        zh, xl = divmod(j, 2)
        one_hot = placing(copy_ref, j).T.astype(BF16)
        at = 64 * xl
        queries = jnp.concatenate(
            [dq[256 * zh + at : 256 * zh + at + 64], dq[256 * zh + 128 + at : 256 * zh + 192 + at]], axis=0
        )
        keys = jnp.concatenate(
            [dkvn_ref[128 * zh + at : 128 * zh + at + 64, :], dkv[128 * zh + at : 128 * zh + at + 64]], axis=0
        )
        moved = contract(one_hot, jnp.concatenate([queries, keys], axis=1), 1, 0).astype(BF16)
        for z in range(4):
            for i in range(3):
                out_ref[4 * z + j, 32 * i : 32 * i + 32, :] = moved[32 * z : 32 * z + 32, HD * i : HD * (i + 1)]


def unpack_kernel(got_ref, dq_ref, dk_ref, dv_ref):
    rows = dq_ref.shape[0]
    for h in range(16):
        for i, ref in enumerate((dq_ref, dk_ref, dv_ref)):
            ref[:, h * HD : (h + 1) * HD] = got_ref[h, i * rows : (i + 1) * rows, :]


def swap(x, mask):
    return lax.ppermute(x, QUERY_AXES, [(i, i ^ mask) for i in range(4)])


def swap_y(x, mask):
    return lax.ppermute(x, "y", [(i, i ^ mask) for i in range(4)])


def shape(dims, dtype=BF16):
    return jax.ShapeDtypeStruct(dims, dtype)


def per_device(query_in, key_in, value_in, saved_out, grad_out, saved_lse, row_block, row_copy):
    copies = row_copy.reshape(-1, RUN)
    ids = row_block[:: 4 * RUN]
    rows = query_in.shape[0]
    packed = call(
        pack_kernel,
        shape((16, 4 * rows + 16, HD)),
        (query_in, key_in, value_in, saved_out, grad_out, saved_lse.T),
        hbm=range(6),
        limit=62 << 20,
        scratch=[pltpu.VMEM(query_in.shape, BF16)] * 5 + [pltpu.VMEM((4, 128), F32), pltpu.SemaphoreType.DMA((6,))],
    )
    got = lax.all_to_all(packed, HEAD_AXES, 0, 0, tiled=True)
    qd, kv, kvn = call(
        sort_kernel, (shape((528, 256)), shape((4, 256, 256)), shape((256, 256))), (got, copies)
    )
    qd2 = swap(qd, 2)
    kvs = lax.all_to_all(kv, "y", 0, 0, tiled=True)
    qd1 = swap(qd, 1)
    qd3 = swap(qd2, 1)
    outs = (
        (shape((2, 512, HD), F32), shape((2, 512, HD)), shape((256, 256), F32)) + (shape((256, 256)),) * 4
    )
    scratch = (
        pltpu.VMEM((4, 512, HD), BF16), pltpu.VMEM((4, 512, HD), BF16),
        pltpu.VMEM((4, 1, 512), F32), pltpu.VMEM((4, 1, 512), F32),
        pltpu.VMEM((1280, HD), BF16), pltpu.VMEM((HD, 1280), BF16), pltpu.VMEM((1280, HD), BF16),
        pltpu.VMEM((1280, HD), F32), pltpu.VMEM((1280, HD), F32),
    )
    dq_keep, dq_send, *dkvs, dkvn = call(
        attend_kernel, outs, (ids, qd, qd1, qd2, qd3, kvs, kvn), smem=(0,), scratch=scratch
    )
    dq_core = swap(dq_send, 1)
    for m in (2, 1, 3):
        dkvs[m] = swap_y(dkvs[m], m)
    dq_chip = swap(call(add_kernel, shape((512, HD)), (dq_keep, dq_core)), 2)
    back = call(unsort_kernel, shape((16, 3 * rows, HD)), (dq_keep, dq_core, dq_chip, *dkvs, dkvn, copies))
    back = lax.all_to_all(back, HEAD_AXES, 0, 0, tiled=True)
    return call(unpack_kernel, (shape((rows, 16 * HD)),) * 3, (back,))


def solution(mesh):
    fine = Mesh(mesh.devices.reshape(SIZES), AXES)
    whole = P(AXES, None)
    return jax.shard_map(
        per_device,
        mesh=fine,
        in_specs=(whole, whole, whole, whole, whole, P(AXES[:5], AXES[5]), P(), P()),
        out_specs=(whole, whole, whole),
        check_vma=False,
    )
```

```python
import jax
import jax.numpy as jnp
from jax import lax
from jax.experimental import pallas as pl
from jax.experimental.pallas import tpu as pltpu
from jax.sharding import Mesh
from jax.sharding import PartitionSpec as P

HD = 128
RUN = 128
HALF = RUN // 2
AXES = ("y", "zh", "xh", "xl", "c", "zl")
SIZES = (4, 2, 2, 2, 2, 4)
HEAD_AXES = ("zl", "zh", "xl")
BACK_AXES = ("zh", "xl", "zl")
QUERY_AXES = ("xh", "c")
RUNS = 4
SCALE = HD**-0.5
LOG2E = 1.4426950408889634
OFF = 1e30
F32 = jnp.float32
BF16 = jnp.bfloat16
VMEM = pl.BlockSpec(memory_space=pltpu.VMEM)
HBM = pl.BlockSpec(memory_space=pltpu.HBM)
SMEM = pl.BlockSpec(memory_space=pltpu.SMEM)


def iota(shape, axis):
    return lax.broadcasted_iota(jnp.int32, shape, axis)


def split_two(x):
    high = x.astype(BF16).astype(F32)
    return high, x - high


def contract(a, b, dim_a, dim_b):
    return lax.dot_general(a, b, (((dim_a,), (dim_b,)), ((), ())), preferred_element_type=F32)


def call(body, out_shape, args, smem=(), hbm=(), scratch=(), limit=32 << 20, cost=None):
    return pl.pallas_call(
        body,
        out_shape=out_shape,
        in_specs=[SMEM if i in smem else HBM if i in hbm else VMEM for i in range(len(args))],
        out_specs=jax.tree.map(lambda _: VMEM, out_shape),
        scratch_shapes=list(scratch),
        compiler_params=pltpu.CompilerParams(vmem_limit_bytes=limit),
        cost_estimate=cost,
    )(*args)


def pack_kernel(q_in, k_in, v_in, o_in, g_in, lse_in, out_ref, q_ref, k_ref, v_ref, o_ref, g_ref, lse_ref, sems):
    pairs = ((g_in, g_ref), (o_in, o_ref), (lse_in, lse_ref), (q_in, q_ref), (k_in, k_ref), (v_in, v_ref))
    copies = [pltpu.make_async_copy(a, b, sems.at[i]) for i, (a, b) in enumerate(pairs)]
    for copy in copies:
        copy.start()
    rows = q_ref.shape[0]
    for copy in copies[:3]:
        copy.wait()
    lane = iota((rows, 128), 1)
    delta = jnp.zeros((rows, 128), F32)
    for h in range(16):
        cols = slice(h * HD, (h + 1) * HD)
        term = g_ref[:, cols].astype(F32) * o_ref[:, cols].astype(F32)
        delta = jnp.where(lane == h, jnp.sum(term, axis=1, keepdims=True), delta)
    delta = jnp.concatenate([delta, jnp.zeros((128 - rows, 128), F32)], axis=0).T
    delta_high, delta_low = split_two(delta)
    lse_high, lse_low = split_two(lse_ref[...])
    row = iota((8, 128), 0)
    for copy in copies[3:]:
        copy.wait()
    for h in range(16):
        j = h % 4
        cols = slice(h * HD, (h + 1) * HD)
        for i, ref in enumerate((q_ref, g_ref, k_ref, v_ref)):
            out_ref[h, i * rows : (i + 1) * rows, :] = ref[:, cols]
        stats = jnp.where(row == 0, lse_high[j : j + 1], 0.0)
        stats = jnp.where(row == 1, lse_low[j : j + 1], stats)
        stats = jnp.where(row == 2, delta_high[h : h + 1], stats)
        stats = jnp.where(row == 3, delta_low[h : h + 1], stats)
        out_ref[h, 4 * rows : 4 * rows + 8, :] = stats.astype(BF16)


def placing(copy_ref, j):
    zh, xl = divmod(j, 2)
    shard = ((lax.axis_index("y") * 2 + zh) * 4 + lax.axis_index("xh") * 2 + xl) * 2 + lax.axis_index("c")
    copy = jnp.broadcast_to(copy_ref[pl.ds(shard, 1), :], (8, RUN)).astype(F32)
    upto = (iota((RUN, RUN), 0) <= iota((RUN, RUN), 1)).astype(BF16)
    count = contract(copy.astype(BF16), upto, 1, 0)
    index = iota((8, RUN), 1).astype(F32)
    place = jnp.where(copy > 0.5, HALF - 1.0 + count, index - count)
    place = jnp.broadcast_to(place[0:1], (RUN, RUN)).astype(jnp.int32)
    return (iota((RUN, RUN), 0) == place).astype(F32)


def sort_kernel(got_ref, copy_ref, qd_ref, kv_ref, kvn_ref):
    zl = lax.axis_index("zl")
    row = iota((8, RUN), 0)
    stats = []
    for j in range(RUNS):
        zh, xl = divmod(j, 2)
        one_hot = placing(copy_ref, j).astype(BF16)
        parts = [
            jnp.concatenate([got_ref[4 * z + j, 32 * i : 32 * i + 32, :] for z in range(4)], axis=0)
            for i in range(4)
        ]
        moved = contract(one_hot, jnp.concatenate(parts, axis=1), 1, 0).astype(BF16)
        qd_ref[256 * zh + 64 * xl : 256 * zh + 64 * xl + 64, :] = moved[:HALF, :256]
        qd_ref[256 * zh + 128 + 64 * xl : 256 * zh + 192 + 64 * xl, :] = moved[HALF:, :256]
        kvn_ref[128 * zh + 64 * xl : 128 * zh + 64 * xl + 64, :] = moved[:HALF, 256:]
        for y in range(4):
            kv_ref[y, 128 * zh + 64 * xl : 128 * zh + 64 * xl + 64, :] = moved[HALF:, 256:]
        lse = got_ref[4 * zl + j, 128:136, :].astype(F32)
        delta = jnp.concatenate(
            [got_ref[4 * z + j, 128:136, :].astype(F32)[:, :32] for z in range(4)], axis=1
        )
        both = jnp.where(row < 2, lse, delta)
        both = jnp.concatenate([both, jnp.zeros_like(both)], axis=0).astype(BF16)
        stats.append(contract(both, one_hot, 1, 1))
    halves = []
    for zh in range(2):
        a, b = stats[2 * zh], stats[2 * zh + 1]
        halves.append(
            jnp.concatenate([a[:8, :HALF], b[:8, :HALF], a[:8, HALF:], b[:8, HALF:]], axis=1)
        )
    qd_ref[512:528, :] = jnp.concatenate(halves, axis=0).astype(BF16)


def attend_kernel(
    ids_ref, qd0, qd1, qd2, qd3, kv_ref, kvn_ref,
    dq_keep, dq_send, dkv0, dkv1, dkv2, dkv3, dkvn_ref,
    q_all, g_all, lse_all, delta_all, k_all, kt_all, v_all, dk_all, dv_all,
):
    y, xh = lax.axis_index("y"), lax.axis_index("xh")
    for m, ref in enumerate((qd0, qd1, qd2, qd3)):
        stats = ref[512:528, :].astype(F32)
        for zh in range(2):
            block, at = zh * 2 + m // 2, 256 * (m % 2)
            q_all[block, at : at + 256, :] = ref[256 * zh : 256 * zh + 256, :HD]
            g_all[block, at : at + 256, :] = ref[256 * zh : 256 * zh + 256, HD:]
            s = 8 * zh
            lse_all[block, :, at : at + 256] = (stats[s : s + 1] + stats[s + 1 : s + 2]) * LOG2E
            delta_all[block, :, at : at + 256] = stats[s + 2 : s + 3] + stats[s + 3 : s + 4]
    for first, ref in ((0, kvn_ref.at[:128]), (1152, kvn_ref.at[128:])) + tuple(
        (128 + 256 * d, kv_ref.at[d]) for d in range(4)
    ):
        size = ref.shape[0]
        k = ref[:, :HD]
        k_all[first : first + size, :] = k
        v_all[first : first + size, :] = ref[:, HD:]
        kt_all[:, first : first + size] = k.astype(F32).T.astype(BF16)

    clean = iota((1, 512), 1) // 128 % 2 == 1
    for block in (1, 3, 0, 2):
        zh, other = divmod(block, 2)
        own_id = ids_ref[(y * 2 + zh) * 2 + (xh ^ other)]
        lse, delta = lse_all[block], delta_all[block]
        limits = []
        for n in range(8):
            key_id = ids_ref[2 * n + xh]
            noisy_off = jnp.where(key_id < own_id, 0.0, OFF)
            clean_off = jnp.where(key_id <= own_id, 0.0, OFF)
            limits.append(lse + jnp.where(clean, clean_off, noisy_off))
        first, last = 128, 1152
        if not other:
            own_noisy = lse + jnp.where(clean, OFF, 0.0)
            limits = limits + [own_noisy] if zh else [own_noisy] + limits
            first, last = (128, 1280) if zh else (0, 1152)
        q, g = q_all[block], g_all[block]
        scores = contract(k_all[first:last, :], q, 1, 1)
        weights = jnp.concatenate(
            [jnp.exp2(scores[128 * i : 128 * i + 128] * (SCALE * LOG2E) - row) for i, row in enumerate(limits)],
            axis=0,
        )
        dweights = contract(v_all[first:last, :], g, 1, 1)
        dscores = (weights * (dweights - delta)).astype(BF16)
        dv = contract(weights.astype(BF16), g, 1, 0)
        dk = contract(dscores, q, 1, 0)
        if block == 1:
            dk_all[first:last, :] = dk
            dv_all[first:last, :] = dv
            zeros = jnp.zeros((128, HD), F32)
            for ref in (dk_all, dv_all):
                ref[:128, :] = zeros
                ref[1152:, :] = zeros
        else:
            dk_all[first:last, :] += dk
            dv_all[first:last, :] += dv
        dq = contract(kt_all[:, first:last], dscores, 1, 0).T * SCALE
        dq_keep[other, 256 * zh : 256 * zh + 256, :] = dq[:256]
        dq_send[other, 256 * zh : 256 * zh + 256, :] = dq[256:].astype(BF16)
    pieces = [(0, dkvn_ref.at[:128]), (1152, dkvn_ref.at[128:])]
    for m, ref in enumerate((dkv0, dkv1, dkv2, dkv3)):
        pieces.append((pl.multiple_of(128 + 256 * (y ^ m), 128), ref))
    for first, ref in pieces:
        rows = pl.ds(first, ref.shape[0])
        ref[:, :HD] = (dk_all[rows, :] * SCALE).astype(ref.dtype)
        ref[:, HD:] = dv_all[rows, :].astype(ref.dtype)


def add_kernel(keep_ref, got_ref, out_ref):
    out_ref[...] = (keep_ref[1] + got_ref[1].astype(F32)).astype(BF16)


def unsort_kernel(keep_ref, got_core, got_chip, dkv0, dkv1, dkv2, dkv3, dkvn_ref, copy_ref, out_ref):
    dq = (keep_ref[0] + got_core[0].astype(F32) + got_chip[...].astype(F32)).astype(BF16)
    dkv = (dkv0[...] + dkv1[...].astype(F32) + dkv2[...].astype(F32) + dkv3[...].astype(F32)).astype(BF16)
    for j in range(RUNS):
        zh, xl = divmod(j, 2)
        one_hot = placing(copy_ref, j).T.astype(BF16)
        at = 64 * xl
        queries = jnp.concatenate(
            [dq[256 * zh + at : 256 * zh + at + 64], dq[256 * zh + 128 + at : 256 * zh + 192 + at]], axis=0
        )
        keys = jnp.concatenate(
            [dkvn_ref[128 * zh + at : 128 * zh + at + 64, :], dkv[128 * zh + at : 128 * zh + at + 64]], axis=0
        )
        moved = contract(one_hot, jnp.concatenate([queries, keys], axis=1), 1, 0).astype(BF16)
        for z in range(4):
            for i in range(3):
                out_ref[4 * j + z, 32 * i : 32 * i + 32, :] = moved[32 * z : 32 * z + 32, HD * i : HD * (i + 1)]


def unpack_kernel(got_ref, dq_ref, dk_ref, dv_ref):
    rows = dq_ref.shape[0]
    for h in range(16):
        for i, ref in enumerate((dq_ref, dk_ref, dv_ref)):
            ref[:, h * HD : (h + 1) * HD] = got_ref[4 * (h % 4) + h // 4, i * rows : (i + 1) * rows, :]


def swap(x, mask):
    return lax.ppermute(x, QUERY_AXES, [(i, i ^ mask) for i in range(4)])


def swap_y(x, mask):
    return lax.ppermute(x, "y", [(i, i ^ mask) for i in range(4)])


def shape(dims, dtype=BF16):
    return jax.ShapeDtypeStruct(dims, dtype)


def per_device(query_in, key_in, value_in, saved_out, grad_out, saved_lse, row_block, row_copy):
    copies = row_copy.reshape(-1, RUN)
    ids = row_block[:: 4 * RUN]
    rows = query_in.shape[0]
    packed = call(
        pack_kernel,
        shape((16, 4 * rows + 8, HD)),
        (query_in, key_in, value_in, saved_out, grad_out, saved_lse.T),
        hbm=range(6),
        limit=62 << 20,
        scratch=[pltpu.VMEM(query_in.shape, BF16)] * 5 + [pltpu.VMEM((4, 128), F32), pltpu.SemaphoreType.DMA((6,))],
    )
    got = lax.all_to_all(packed, HEAD_AXES, 0, 0, tiled=True)
    qd, kv, kvn = call(
        sort_kernel, (shape((528, 256)), shape((4, 256, 256)), shape((256, 256))), (got, copies)
    )
    qd2 = swap(qd, 2)
    kvs = lax.all_to_all(kv, "y", 0, 0, tiled=True)
    qd1 = swap(qd, 1)
    qd3 = swap(qd2, 1)
    outs = (
        (shape((2, 512, HD), F32), shape((2, 512, HD)), shape((256, 256), F32)) + (shape((256, 256)),) * 4
    )
    scratch = (
        pltpu.VMEM((4, 512, HD), BF16), pltpu.VMEM((4, 512, HD), BF16),
        pltpu.VMEM((4, 1, 512), F32), pltpu.VMEM((4, 1, 512), F32),
        pltpu.VMEM((1280, HD), BF16), pltpu.VMEM((HD, 1280), BF16), pltpu.VMEM((1280, HD), BF16),
        pltpu.VMEM((1280, HD), F32), pltpu.VMEM((1280, HD), F32),
    )
    dq_keep, dq_send, *dkvs, dkvn = call(
        attend_kernel, outs, (ids, qd, qd1, qd2, qd3, kvs, kvn), smem=(0,), scratch=scratch
    )
    dq_core = swap(dq_send, 1)
    for m in (2, 1, 3):
        dkvs[m] = swap_y(dkvs[m], m)
    dq_chip = swap(call(add_kernel, shape((512, HD)), (dq_keep, dq_core)), 2)
    back = call(unsort_kernel, shape((16, 3 * rows, HD)), (dq_keep, dq_core, dq_chip, *dkvs, dkvn, copies))
    back = lax.all_to_all(back, BACK_AXES, 0, 0, tiled=True)
    return call(unpack_kernel, (shape((rows, 16 * HD)),) * 3, (back,))


def solution(mesh):
    fine = Mesh(mesh.devices.reshape(SIZES), AXES)
    whole = P(AXES, None)
    return jax.shard_map(
        per_device,
        mesh=fine,
        in_specs=(whole, whole, whole, whole, whole, P(AXES[:5], AXES[5]), P(), P()),
        out_specs=(whole, whole, whole),
        check_vma=False,
    )
```

```python
import jax
import jax.numpy as jnp
from jax import lax
from jax.experimental import pallas as pl
from jax.experimental.pallas import tpu as pltpu
from jax.sharding import Mesh
from jax.sharding import PartitionSpec as P

HD = 128
RUN = 128
HALF = RUN // 2
AXES = ("y", "zh", "xh", "xl", "c", "zl")
SIZES = (4, 2, 2, 2, 2, 4)
HEAD_AXES = ("zl", "zh", "xl")
BACK_AXES = ("zh", "xl", "zl")
QUERY_AXES = ("xh", "c")
RUNS = 4
SCALE = HD**-0.5
LOG2E = 1.4426950408889634
OFF = 1e30
F32 = jnp.float32
BF16 = jnp.bfloat16
VMEM = pl.BlockSpec(memory_space=pltpu.VMEM)
HBM = pl.BlockSpec(memory_space=pltpu.HBM)
SMEM = pl.BlockSpec(memory_space=pltpu.SMEM)


def iota(shape, axis):
    return lax.broadcasted_iota(jnp.int32, shape, axis)


def split_two(x):
    high = x.astype(BF16).astype(F32)
    return high, x - high


def contract(a, b, dim_a, dim_b):
    return lax.dot_general(a, b, (((dim_a,), (dim_b,)), ((), ())), preferred_element_type=F32)


def call(body, out_shape, args, smem=(), hbm=(), scratch=(), limit=32 << 20, cost=None):
    return pl.pallas_call(
        body,
        out_shape=out_shape,
        in_specs=[SMEM if i in smem else HBM if i in hbm else VMEM for i in range(len(args))],
        out_specs=jax.tree.map(lambda _: VMEM, out_shape),
        scratch_shapes=list(scratch),
        compiler_params=pltpu.CompilerParams(vmem_limit_bytes=limit),
        cost_estimate=cost,
    )(*args)


def pack_kernel(q_in, k_in, v_in, o_in, g_in, lse_in, out_ref, q_ref, k_ref, v_ref, o_ref, g_ref, lse_ref, sems):
    pairs = ((g_in, g_ref), (o_in, o_ref), (lse_in, lse_ref), (q_in, q_ref), (k_in, k_ref), (v_in, v_ref))
    copies = [pltpu.make_async_copy(a, b, sems.at[i]) for i, (a, b) in enumerate(pairs)]
    for copy in copies:
        copy.start()
    rows = q_ref.shape[0]
    for copy in copies[:3]:
        copy.wait()
    lane = iota((rows, 128), 1)
    delta = jnp.zeros((rows, 128), F32)
    for h in range(16):
        cols = slice(h * HD, (h + 1) * HD)
        term = g_ref[:, cols].astype(F32) * o_ref[:, cols].astype(F32)
        delta = jnp.where(lane == h, jnp.sum(term, axis=1, keepdims=True), delta)
    delta = jnp.concatenate([delta, jnp.zeros((128 - rows, 128), F32)], axis=0).T
    delta_high, delta_low = split_two(delta)
    lse_high, lse_low = split_two(lse_ref[...])
    row = iota((8, 128), 0)
    for copy in copies[3:]:
        copy.wait()
    for h in range(16):
        j = h % 4
        cols = slice(h * HD, (h + 1) * HD)
        for i, ref in enumerate((q_ref, g_ref, k_ref, v_ref)):
            out_ref[h, i * rows : (i + 1) * rows, :] = ref[:, cols]
        stats = jnp.where(row == 0, lse_high[j : j + 1], 0.0)
        stats = jnp.where(row == 1, lse_low[j : j + 1], stats)
        stats = jnp.where(row == 2, delta_high[h : h + 1], stats)
        stats = jnp.where(row == 3, delta_low[h : h + 1], stats)
        out_ref[h, 4 * rows : 4 * rows + 8, :] = stats.astype(BF16)


def placing(copy_ref, j):
    zh, xl = divmod(j, 2)
    shard = ((lax.axis_index("y") * 2 + zh) * 4 + lax.axis_index("xh") * 2 + xl) * 2 + lax.axis_index("c")
    copy = jnp.broadcast_to(copy_ref[pl.ds(shard, 1), :], (8, RUN)).astype(F32)
    upto = (iota((RUN, RUN), 0) <= iota((RUN, RUN), 1)).astype(BF16)
    count = contract(copy.astype(BF16), upto, 1, 0)
    index = iota((8, RUN), 1).astype(F32)
    place = jnp.where(copy > 0.5, HALF - 1.0 + count, index - count)
    place = jnp.broadcast_to(place[0:1], (RUN, RUN)).astype(jnp.int32)
    return (iota((RUN, RUN), 0) == place).astype(F32)


def sort_kernel(got_ref, copy_ref, qd_ref, kv_ref, kvn_ref):
    zl = lax.axis_index("zl")
    row = iota((8, RUN), 0)
    stats = []
    for j in range(RUNS):
        zh, xl = divmod(j, 2)
        one_hot = placing(copy_ref, j).astype(BF16)
        parts = [
            jnp.concatenate([got_ref[4 * z + j, 32 * i : 32 * i + 32, :] for z in range(4)], axis=0)
            for i in range(4)
        ]
        moved = contract(one_hot, jnp.concatenate(parts, axis=1), 1, 0).astype(BF16)
        qd_ref[256 * zh + 64 * xl : 256 * zh + 64 * xl + 64, :] = moved[:HALF, :256]
        qd_ref[256 * zh + 128 + 64 * xl : 256 * zh + 192 + 64 * xl, :] = moved[HALF:, :256]
        kvn_ref[128 * zh + 64 * xl : 128 * zh + 64 * xl + 64, :] = moved[:HALF, 256:]
        for y in range(4):
            kv_ref[y, 128 * zh + 64 * xl : 128 * zh + 64 * xl + 64, :] = moved[HALF:, 256:]
        lse = got_ref[4 * zl + j, 128:136, :].astype(F32)
        delta = jnp.concatenate(
            [got_ref[4 * z + j, 128:136, :].astype(F32)[:, :32] for z in range(4)], axis=1
        )
        both = jnp.where(row < 2, lse, delta)
        both = jnp.concatenate([both, jnp.zeros_like(both)], axis=0).astype(BF16)
        stats.append(contract(both, one_hot, 1, 1))
    halves = []
    for zh in range(2):
        a, b = stats[2 * zh], stats[2 * zh + 1]
        halves.append(
            jnp.concatenate([a[:8, :HALF], b[:8, :HALF], a[:8, HALF:], b[:8, HALF:]], axis=1)
        )
    qd_ref[512:528, :] = jnp.concatenate(halves, axis=0).astype(BF16)


def attend_kernel(
    ids_ref, qd0, qd1, qd2, qd3, kv_ref, kvn_ref,
    dq_keep, dq_send, dkv0, dkv1, dkv2, dkv3, dkvn_ref,
    q_all, g_all, lse_all, delta_all, k_all, kt_all, v_all, dk_all, dv_all,
):
    y, xh = lax.axis_index("y"), lax.axis_index("xh")
    for m, ref in enumerate((qd0, qd1, qd2, qd3)):
        stats = ref[512:528, :].astype(F32)
        for zh in range(2):
            block, at = zh * 2 + m // 2, 256 * (m % 2)
            q_all[block, at : at + 256, :] = ref[256 * zh : 256 * zh + 256, :HD]
            g_all[block, at : at + 256, :] = ref[256 * zh : 256 * zh + 256, HD:]
            s = 8 * zh
            lse_all[block, :, at : at + 256] = (stats[s : s + 1] + stats[s + 1 : s + 2]) * LOG2E
            delta_all[block, :, at : at + 256] = stats[s + 2 : s + 3] + stats[s + 3 : s + 4]
    for first, ref in ((0, kvn_ref.at[:128]), (1152, kvn_ref.at[128:])) + tuple(
        (128 + 256 * d, kv_ref.at[d]) for d in range(4)
    ):
        size = ref.shape[0]
        k = ref[:, :HD]
        k_all[first : first + size, :] = k
        v_all[first : first + size, :] = ref[:, HD:]
        kt_all[:, first : first + size] = k.astype(F32).T.astype(BF16)

    clean = iota((1, 512), 1) // 128 % 2 == 1
    for block in (1, 3, 0, 2):
        zh, other = divmod(block, 2)
        own_id = ids_ref[(y * 2 + zh) * 2 + (xh ^ other)]
        lse, delta = lse_all[block], delta_all[block]
        limits = []
        for n in range(8):
            key_id = ids_ref[2 * n + xh]
            noisy_off = jnp.where(key_id < own_id, 0.0, OFF)
            clean_off = jnp.where(key_id <= own_id, 0.0, OFF)
            limits.append(lse + jnp.where(clean, clean_off, noisy_off))
        first, last = 128, 1152
        if not other:
            own_noisy = lse + jnp.where(clean, OFF, 0.0)
            limits = limits + [own_noisy] if zh else [own_noisy] + limits
            first, last = (128, 1280) if zh else (0, 1152)
        q, g = q_all[block], g_all[block]
        scores = contract(k_all[first:last, :], q, 1, 1)
        weights = jnp.concatenate(
            [jnp.exp2(scores[128 * i : 128 * i + 128] * (SCALE * LOG2E) - row) for i, row in enumerate(limits)],
            axis=0,
        )
        dweights = contract(v_all[first:last, :], g, 1, 1)
        dscores = (weights * (dweights - delta)).astype(BF16)
        dv = contract(weights.astype(BF16), g, 1, 0)
        dk = contract(dscores, q, 1, 0)
        if block == 1:
            dk_all[first:last, :] = dk
            dv_all[first:last, :] = dv
            zeros = jnp.zeros((128, HD), F32)
            for ref in (dk_all, dv_all):
                ref[:128, :] = zeros
                ref[1152:, :] = zeros
        else:
            dk_all[first:last, :] += dk
            dv_all[first:last, :] += dv
        dq = contract(kt_all[:, first:last], dscores, 1, 0).T * SCALE
        dq_keep[other, 256 * zh : 256 * zh + 256, :] = dq[:256]
        dq_send[other, 256 * zh : 256 * zh + 256, :] = dq[256:].astype(BF16)
    pieces = [(0, dkvn_ref.at[:128]), (1152, dkvn_ref.at[128:])]
    for m, ref in enumerate((dkv0, dkv1, dkv2, dkv3)):
        pieces.append((pl.multiple_of(128 + 256 * (y ^ m), 128), ref))
    for first, ref in pieces:
        rows = pl.ds(first, ref.shape[0])
        ref[:, :HD] = (dk_all[rows, :] * SCALE).astype(ref.dtype)
        ref[:, HD:] = dv_all[rows, :].astype(ref.dtype)


def add_kernel(keep_ref, got_ref, out_ref):
    out_ref[...] = (keep_ref[1] + got_ref[1].astype(F32)).astype(BF16)


def unsort_kernel(keep_ref, got_core, got_chip, dkv0, dkv1, dkv2, dkv3, dkvn_ref, copy_ref, out_ref):
    dq = (keep_ref[0] + got_core[0].astype(F32) + got_chip[...].astype(F32)).astype(BF16)
    dkv = (dkv0[...] + dkv1[...].astype(F32) + dkv2[...].astype(F32) + dkv3[...].astype(F32)).astype(BF16)
    for j in range(RUNS):
        zh, xl = divmod(j, 2)
        one_hot = placing(copy_ref, j).T.astype(BF16)
        at = 64 * xl
        queries = jnp.concatenate(
            [dq[256 * zh + at : 256 * zh + at + 64], dq[256 * zh + 128 + at : 256 * zh + 192 + at]], axis=0
        )
        keys = jnp.concatenate(
            [dkvn_ref[128 * zh + at : 128 * zh + at + 64, :], dkv[128 * zh + at : 128 * zh + at + 64]], axis=0
        )
        moved = contract(one_hot, jnp.concatenate([queries, keys], axis=1), 1, 0).astype(BF16)
        for z in range(4):
            for i in range(3):
                out_ref[4 * j + z, 32 * i : 32 * i + 32, :] = moved[32 * z : 32 * z + 32, HD * i : HD * (i + 1)]


def unpack_kernel(got_ref, dq_ref, dk_ref, dv_ref):
    rows = dq_ref.shape[0]
    for h in range(16):
        for i, ref in enumerate((dq_ref, dk_ref, dv_ref)):
            ref[:, h * HD : (h + 1) * HD] = got_ref[4 * (h % 4) + h // 4, i * rows : (i + 1) * rows, :]


def swap(x, mask):
    return lax.ppermute(x, QUERY_AXES, [(i, i ^ mask) for i in range(4)])


def swap_y(x, mask):
    return lax.ppermute(x, "y", [(i, i ^ mask) for i in range(4)])


def shape(dims, dtype=BF16):
    return jax.ShapeDtypeStruct(dims, dtype)


def per_device(query_in, key_in, value_in, saved_out, grad_out, saved_lse, row_block, row_copy):
    copies = row_copy.reshape(-1, RUN)
    ids = row_block[:: 4 * RUN]
    rows = query_in.shape[0]
    arrays = (query_in, key_in, value_in, saved_out, grad_out, saved_lse.T)
    packed = call(
        pack_kernel,
        shape((16, 4 * rows + 8, HD)),
        tuple(pltpu.with_memory_space_constraint(x, pltpu.HBM) for x in arrays),
        hbm=range(6),
        scratch=[pltpu.VMEM(query_in.shape, BF16)] * 5 + [pltpu.VMEM((4, 128), F32), pltpu.SemaphoreType.DMA((6,))],
    )
    got = lax.all_to_all(packed, HEAD_AXES, 0, 0, tiled=True)
    qd, kv, kvn = call(
        sort_kernel, (shape((528, 256)), shape((4, 256, 256)), shape((256, 256))), (got, copies)
    )
    qd2 = swap(qd, 2)
    kvs = lax.all_to_all(kv, "y", 0, 0, tiled=True)
    qd1 = swap(qd, 1)
    qd3 = swap(qd2, 1)
    outs = (
        (shape((2, 512, HD), F32), shape((2, 512, HD)), shape((256, 256), F32)) + (shape((256, 256)),) * 4
    )
    scratch = (
        pltpu.VMEM((4, 512, HD), BF16), pltpu.VMEM((4, 512, HD), BF16),
        pltpu.VMEM((4, 1, 512), F32), pltpu.VMEM((4, 1, 512), F32),
        pltpu.VMEM((1280, HD), BF16), pltpu.VMEM((HD, 1280), BF16), pltpu.VMEM((1280, HD), BF16),
        pltpu.VMEM((1280, HD), F32), pltpu.VMEM((1280, HD), F32),
    )
    dq_keep, dq_send, *dkvs, dkvn = call(
        attend_kernel, outs, (ids, qd, qd1, qd2, qd3, kvs, kvn), smem=(0,), scratch=scratch
    )
    dq_core = swap(dq_send, 1)
    for m in (2, 1, 3):
        dkvs[m] = swap_y(dkvs[m], m)
    dq_chip = swap(call(add_kernel, shape((512, HD)), (dq_keep, dq_core)), 2)
    back = call(unsort_kernel, shape((16, 3 * rows, HD)), (dq_keep, dq_core, dq_chip, dkvs[0], dkvs[3], dkvs[2], dkvs[1], dkvn, copies))
    back = lax.all_to_all(back, BACK_AXES, 0, 0, tiled=True)
    return call(unpack_kernel, (shape((rows, 16 * HD)),) * 3, (back,))


def solution(mesh):
    fine = Mesh(mesh.devices.reshape(SIZES), AXES)
    whole = P(AXES, None)
    return jax.shard_map(
        per_device,
        mesh=fine,
        in_specs=(whole, whole, whole, whole, whole, P(AXES[:5], AXES[5]), P(), P()),
        out_specs=(whole, whole, whole),
        check_vma=False,
    )
```

```python
import jax
import jax.numpy as jnp
from jax import lax
from jax.experimental import pallas as pl
from jax.experimental.pallas import tpu as pltpu
from jax.sharding import Mesh
from jax.sharding import PartitionSpec as P

HD = 128
RUN = 128
HALF = RUN // 2
AXES = ("y", "zh", "xh", "xl", "c", "zl")
SIZES = (4, 2, 2, 2, 2, 4)
HEAD_AXES = ("zl", "zh", "xl")
BACK_AXES = ("zh", "xl", "zl")
QUERY_AXES = ("xh", "c")
RUNS = 4
SCALE = HD**-0.5
LOG2E = 1.4426950408889634
OFF = 1e30
F32 = jnp.float32
BF16 = jnp.bfloat16
VMEM = pl.BlockSpec(memory_space=pltpu.VMEM)
HBM = pl.BlockSpec(memory_space=pltpu.HBM)
SMEM = pl.BlockSpec(memory_space=pltpu.SMEM)


def iota(shape, axis):
    return lax.broadcasted_iota(jnp.int32, shape, axis)


def split_two(x):
    high = x.astype(BF16).astype(F32)
    return high, x - high


def contract(a, b, dim_a, dim_b):
    return lax.dot_general(a, b, (((dim_a,), (dim_b,)), ((), ())), preferred_element_type=F32)


def call(body, out_shape, args, smem=(), hbm=(), scratch=(), limit=32 << 20, cost=None):
    return pl.pallas_call(
        body,
        out_shape=out_shape,
        in_specs=[SMEM if i in smem else HBM if i in hbm else VMEM for i in range(len(args))],
        out_specs=jax.tree.map(lambda _: VMEM, out_shape),
        scratch_shapes=list(scratch),
        compiler_params=pltpu.CompilerParams(vmem_limit_bytes=limit),
        cost_estimate=cost,
    )(*args)


def pack_kernel(q_in, k_in, v_in, o_in, g_in, lse_in, out_ref, q_ref, k_ref, v_ref, o_ref, g_ref, lse_ref, sems):
    pairs = ((g_in, g_ref), (o_in, o_ref), (lse_in, lse_ref), (q_in, q_ref), (k_in, k_ref), (v_in, v_ref))
    copies = [pltpu.make_async_copy(a, b, sems.at[i]) for i, (a, b) in enumerate(pairs)]
    for copy in copies:
        copy.start()
    rows = q_ref.shape[0]
    for copy in copies[:3]:
        copy.wait()
    lane = iota((rows, 128), 1)
    delta = jnp.zeros((rows, 128), F32)
    for h in range(16):
        cols = slice(h * HD, (h + 1) * HD)
        term = g_ref[:, cols].astype(F32) * o_ref[:, cols].astype(F32)
        delta = jnp.where(lane == h, jnp.sum(term, axis=1, keepdims=True), delta)
    delta = jnp.concatenate([delta, jnp.zeros((128 - rows, 128), F32)], axis=0).T
    delta_high, delta_low = split_two(delta)
    lse_high, lse_low = split_two(lse_ref[...])
    row = iota((8, 128), 0)
    for copy in copies[3:]:
        copy.wait()
    for h in range(16):
        j = h % 4
        cols = slice(h * HD, (h + 1) * HD)
        for i, ref in enumerate((q_ref, g_ref, k_ref, v_ref)):
            out_ref[h, i * rows : (i + 1) * rows, :] = ref[:, cols]
        stats = jnp.where(row == 0, lse_high[j : j + 1], 0.0)
        stats = jnp.where(row == 1, lse_low[j : j + 1], stats)
        stats = jnp.where(row == 2, delta_high[h : h + 1], stats)
        stats = jnp.where(row == 3, delta_low[h : h + 1], stats)
        out_ref[h, 4 * rows : 4 * rows + 8, :] = stats.astype(BF16)


def placing(copy_ref, j):
    zh, xl = divmod(j, 2)
    shard = ((lax.axis_index("y") * 2 + zh) * 4 + lax.axis_index("xh") * 2 + xl) * 2 + lax.axis_index("c")
    copy = jnp.broadcast_to(copy_ref[pl.ds(shard, 1), :], (8, RUN)).astype(F32)
    upto = (iota((RUN, RUN), 0) <= iota((RUN, RUN), 1)).astype(BF16)
    count = contract(copy.astype(BF16), upto, 1, 0)
    index = iota((8, RUN), 1).astype(F32)
    place = jnp.where(copy > 0.5, HALF - 1.0 + count, index - count)
    place = jnp.broadcast_to(place[0:1], (RUN, RUN)).astype(jnp.int32)
    return (iota((RUN, RUN), 0) == place).astype(F32)


def sort_kernel(got_ref, copy_ref, qd_ref, kv_ref, kvn_ref):
    zl = lax.axis_index("zl")
    row = iota((8, RUN), 0)
    stats = []
    for j in range(RUNS):
        zh, xl = divmod(j, 2)
        one_hot = placing(copy_ref, j).astype(BF16)
        parts = [
            jnp.concatenate([got_ref[4 * z + j, 32 * i : 32 * i + 32, :] for z in range(4)], axis=0)
            for i in range(4)
        ]
        moved = contract(one_hot, jnp.concatenate(parts, axis=1), 1, 0).astype(BF16)
        qd_ref[256 * zh + 64 * xl : 256 * zh + 64 * xl + 64, :] = moved[:HALF, :256]
        qd_ref[256 * zh + 128 + 64 * xl : 256 * zh + 192 + 64 * xl, :] = moved[HALF:, :256]
        kvn_ref[128 * zh + 64 * xl : 128 * zh + 64 * xl + 64, :] = moved[:HALF, 256:]
        kv_ref[128 * zh + 64 * xl : 128 * zh + 64 * xl + 64, :] = moved[HALF:, 256:]
        lse = got_ref[4 * zl + j, 128:136, :].astype(F32)
        delta = jnp.concatenate(
            [got_ref[4 * z + j, 128:136, :].astype(F32)[:, :32] for z in range(4)], axis=1
        )
        both = jnp.where(row < 2, lse, delta)
        both = jnp.concatenate([both, jnp.zeros_like(both)], axis=0).astype(BF16)
        stats.append(contract(both, one_hot, 1, 1))
    halves = []
    for zh in range(2):
        a, b = stats[2 * zh], stats[2 * zh + 1]
        halves.append(
            jnp.concatenate([a[:8, :HALF], b[:8, :HALF], a[:8, HALF:], b[:8, HALF:]], axis=1)
        )
    qd_ref[512:528, :] = jnp.concatenate(halves, axis=0).astype(BF16)


def load_keys(clean, noisy_ref, k_all, kt_all, v_all):
    for m, ref in enumerate((*clean, noisy_ref)):
        rows = slice(256 * m, 256 * m + 256)
        k = ref[:, :HD]
        k_all[rows, :] = k
        v_all[rows, :] = ref[:, HD:]
        kt_all[:, rows] = k.astype(F32).T.astype(BF16)


def attend(ids_ref, qd_ref, other, k_all, kt_all, v_all):
    y, xh = lax.axis_index("y"), lax.axis_index("xh")
    stats = qd_ref[512:528, :].astype(F32)
    lse = jnp.concatenate([stats[0:1] + stats[1:2], stats[8:9] + stats[9:10]], axis=1) * LOG2E
    delta = jnp.concatenate([stats[2:3] + stats[3:4], stats[10:11] + stats[11:12]], axis=1)
    lane = iota((1, 512), 1)
    clean, second = lane // 128 % 2 == 1, lane >= 256
    own_ids = [ids_ref[(y * 2 + zh) * 2 + (xh ^ other)] for zh in range(2)]
    limits = []
    for n in range(8):
        key_id = ids_ref[((y ^ (n // 2)) * 2 + n % 2) * 2 + xh]
        noisy_off, clean_off = (
            jnp.where(second, *(jnp.where(hit, 0.0, OFF) for hit in hits))
            for hits in ([key_id < i for i in own_ids[::-1]], [key_id <= i for i in own_ids[::-1]])
        )
        limits.append(lse + jnp.where(clean, clean_off, noisy_off))
    if not other:
        limits.append(lse + jnp.where(clean | second, OFF, 0.0))
        limits.append(lse + jnp.where(clean | ~second, OFF, 0.0))
    last = 128 * len(limits)
    q, g = qd_ref[:512, :HD], qd_ref[:512, HD:]
    scores = contract(k_all[:last, :], q, 1, 1)
    weights = jnp.concatenate(
        [jnp.exp2(scores[128 * i : 128 * i + 128] * (SCALE * LOG2E) - row) for i, row in enumerate(limits)], axis=0
    )
    dweights = contract(v_all[:last, :], g, 1, 1)
    dscores = (weights * (dweights - delta)).astype(BF16)
    dv = contract(weights.astype(BF16), g, 1, 0)
    dk = contract(dscores, q, 1, 0)
    return dk, dv, contract(kt_all[:, :last], dscores, 1, 0).T * SCALE


def first_kernel(ids_ref, qd0, qd2, kv0, kv1, kv2, kv3, kvn_ref, dq_ref, dk_ref, dv_ref, k_all, kt_all, v_all):
    load_keys((kv0, kv1, kv2, kv3), kvn_ref, k_all, kt_all, v_all)
    dk_ref[...], dv_ref[...], dq_ref[0] = attend(ids_ref, qd0, 0, k_all, kt_all, v_all)
    dk, dv, dq_ref[1] = attend(ids_ref, qd2, 1, k_all, kt_all, v_all)
    dk_ref[:1024, :] += dk
    dv_ref[:1024, :] += dv


def second_kernel(
    ids_ref, qd1, qd3, kv0, kv1, kv2, kv3, kvn_ref, dk_ref, dv_ref,
    dq_ref, dkv0, dkv1, dkv2, dkv3, dkvn, k_all, kt_all, v_all,
):
    load_keys((kv0, kv1, kv2, kv3), kvn_ref, k_all, kt_all, v_all)
    near_dk, near_dv, dq = attend(ids_ref, qd1, 0, k_all, kt_all, v_all)
    dq_ref[0] = dq.astype(BF16)
    far_dk, far_dv, dq = attend(ids_ref, qd3, 1, k_all, kt_all, v_all)
    dq_ref[1] = dq.astype(BF16)
    for m, ref in enumerate((dkv0, dkv1, dkv2, dkv3, dkvn)):
        rows = slice(256 * m, 256 * m + 256)
        dk, dv = dk_ref[rows, :] + near_dk[rows], dv_ref[rows, :] + near_dv[rows]
        if m < 4:
            dk, dv = dk + far_dk[rows], dv + far_dv[rows]
        ref[:, :HD] = (dk * SCALE).astype(ref.dtype)
        ref[:, HD:] = dv.astype(ref.dtype)


def add_kernel(keep_ref, got_ref, out_ref):
    out_ref[...] = (keep_ref[1] + got_ref[1].astype(F32)).astype(BF16)


def unsort_kernel(keep_ref, got_core, got_chip, dkv0, dkv1, dkv2, dkv3, dkvn_ref, copy_ref, out_ref):
    dq = (keep_ref[0] + got_core[0].astype(F32) + got_chip[...].astype(F32)).astype(BF16)
    dkv = (dkv0[...] + dkv1[...].astype(F32) + dkv2[...].astype(F32) + dkv3[...].astype(F32)).astype(BF16)
    for j in range(RUNS):
        zh, xl = divmod(j, 2)
        one_hot = placing(copy_ref, j).T.astype(BF16)
        at = 64 * xl
        queries = jnp.concatenate(
            [dq[256 * zh + at : 256 * zh + at + 64], dq[256 * zh + 128 + at : 256 * zh + 192 + at]], axis=0
        )
        keys = jnp.concatenate(
            [dkvn_ref[128 * zh + at : 128 * zh + at + 64, :], dkv[128 * zh + at : 128 * zh + at + 64]], axis=0
        )
        moved = contract(one_hot, jnp.concatenate([queries, keys], axis=1), 1, 0).astype(BF16)
        for z in range(4):
            for i in range(3):
                out_ref[4 * j + z, 32 * i : 32 * i + 32, :] = moved[32 * z : 32 * z + 32, HD * i : HD * (i + 1)]


def unpack_kernel(got_ref, dq_ref, dk_ref, dv_ref):
    rows = dq_ref.shape[0]
    for h in range(16):
        for i, ref in enumerate((dq_ref, dk_ref, dv_ref)):
            ref[:, h * HD : (h + 1) * HD] = got_ref[4 * (h % 4) + h // 4, i * rows : (i + 1) * rows, :]


def swap(x, mask):
    return lax.ppermute(x, QUERY_AXES, [(i, i ^ mask) for i in range(4)])


def swap_y(x, mask):
    return lax.ppermute(x, "y", [(i, i ^ mask) for i in range(4)])


def shape(dims, dtype=BF16):
    return jax.ShapeDtypeStruct(dims, dtype)


def per_device(query_in, key_in, value_in, saved_out, grad_out, saved_lse, row_block, row_copy):
    copies = row_copy.reshape(-1, RUN)
    ids = row_block[:: 4 * RUN]
    rows = query_in.shape[0]
    arrays = (query_in, key_in, value_in, saved_out, grad_out, saved_lse.T)
    packed = call(
        pack_kernel,
        shape((16, 4 * rows + 8, HD)),
        tuple(pltpu.with_memory_space_constraint(x, pltpu.HBM) for x in arrays),
        hbm=range(6),
        scratch=[pltpu.VMEM(query_in.shape, BF16)] * 5 + [pltpu.VMEM((4, 128), F32), pltpu.SemaphoreType.DMA((6,))],
    )
    got = lax.all_to_all(packed, HEAD_AXES, 0, 0, tiled=True)
    qd, kv, kvn = call(
        sort_kernel, (shape((528, 256)), shape((256, 256)), shape((256, 256))), (got, copies)
    )
    qd2 = swap(qd, 2)
    kv1, kv2, kv3 = (swap_y(kv, m) for m in (1, 2, 3))
    qd2, kv1, kv2, kv3, ids, qd = lax.optimization_barrier((qd2, kv1, kv2, kv3, ids, qd))
    qd1 = swap(qd, 1)
    qd3 = swap(qd2, 1)
    keys = (kv, kv1, kv2, kv3, kvn)
    scratch = (pltpu.VMEM((1280, HD), BF16), pltpu.VMEM((HD, 1280), BF16), pltpu.VMEM((1280, HD), BF16))
    total = shape((1280, HD), F32)
    dq_keep, dk, dv = call(
        first_kernel,
        (shape((2, 512, HD), F32), total, total),
        (ids, qd, qd2, *keys),
        smem=(0,),
        scratch=scratch,
    )
    dq_send, *dkvs, dkvn = call(
        second_kernel,
        (shape((2, 512, HD)), shape((256, 256), F32)) + (shape((256, 256)),) * 4,
        (ids, qd1, qd3, *keys, dk, dv),
        smem=(0,),
        scratch=scratch,
    )
    dq_core = swap(dq_send, 1)
    for m in (2, 1, 3):
        dkvs[m] = swap_y(dkvs[m], m)
    dq_chip = swap(call(add_kernel, shape((512, HD)), (dq_keep, dq_core)), 2)
    back = call(unsort_kernel, shape((16, 3 * rows, HD)), (dq_keep, dq_core, dq_chip, dkvs[0], dkvs[3], dkvs[2], dkvs[1], dkvn, copies))
    back = lax.all_to_all(back, BACK_AXES, 0, 0, tiled=True)
    return call(unpack_kernel, (shape((rows, 16 * HD)),) * 3, (back,))


def solution(mesh):
    fine = Mesh(mesh.devices.reshape(SIZES), AXES)
    whole = P(AXES, None)
    return jax.shard_map(
        per_device,
        mesh=fine,
        in_specs=(whole, whole, whole, whole, whole, P(AXES[:5], AXES[5]), P(), P()),
        out_specs=(whole, whole, whole),
        check_vma=False,
    )
```

```python
import jax
import jax.numpy as jnp
from jax import lax
from jax.experimental import pallas as pl
from jax.experimental.pallas import tpu as pltpu
from jax.sharding import Mesh
from jax.sharding import PartitionSpec as P

HD = 128
RUN = 128
HALF = RUN // 2
AXES = ("y", "zh", "xh", "xl", "c", "zl")
SIZES = (4, 2, 2, 2, 2, 4)
HEAD_AXES = ("zl", "zh", "xl")
BACK_AXES = ("zh", "xl", "zl")
QUERY_AXES = ("xh", "c")
RUNS = 4
SCALE = HD**-0.5
LOG2E = 1.4426950408889634
OFF = 1e30
F32 = jnp.float32
BF16 = jnp.bfloat16
VMEM = pl.BlockSpec(memory_space=pltpu.VMEM)
HBM = pl.BlockSpec(memory_space=pltpu.HBM)
SMEM = pl.BlockSpec(memory_space=pltpu.SMEM)


def iota(shape, axis):
    return lax.broadcasted_iota(jnp.int32, shape, axis)


def split_two(x):
    high = x.astype(BF16).astype(F32)
    return high, x - high


def contract(a, b, dim_a, dim_b):
    return lax.dot_general(a, b, (((dim_a,), (dim_b,)), ((), ())), preferred_element_type=F32)


def call(body, out_shape, args, smem=(), hbm=(), scratch=(), limit=32 << 20, cost=None):
    return pl.pallas_call(
        body,
        out_shape=out_shape,
        in_specs=[SMEM if i in smem else HBM if i in hbm else VMEM for i in range(len(args))],
        out_specs=jax.tree.map(lambda _: VMEM, out_shape),
        scratch_shapes=list(scratch),
        compiler_params=pltpu.CompilerParams(vmem_limit_bytes=limit),
        cost_estimate=cost,
    )(*args)


def pack_kernel(q_in, k_in, v_in, o_in, g_in, lse_in, out_ref, q_ref, k_ref, v_ref, o_ref, g_ref, lse_ref, sems):
    pairs = ((g_in, g_ref), (o_in, o_ref), (lse_in, lse_ref), (q_in, q_ref), (k_in, k_ref), (v_in, v_ref))
    copies = [pltpu.make_async_copy(a, b, sems.at[i]) for i, (a, b) in enumerate(pairs)]
    for copy in copies:
        copy.start()
    rows = q_ref.shape[0]
    for copy in copies[:3]:
        copy.wait()
    lane = iota((rows, 128), 1)
    delta = jnp.zeros((rows, 128), F32)
    for h in range(16):
        cols = slice(h * HD, (h + 1) * HD)
        term = g_ref[:, cols].astype(F32) * o_ref[:, cols].astype(F32)
        delta = jnp.where(lane == h, jnp.sum(term, axis=1, keepdims=True), delta)
    delta = jnp.concatenate([delta, jnp.zeros((128 - rows, 128), F32)], axis=0).T
    delta_high, delta_low = split_two(delta)
    lse_high, lse_low = split_two(lse_ref[...])
    row = iota((8, 128), 0)
    for copy in copies[3:]:
        copy.wait()
    for h in range(16):
        j = h % 4
        cols = slice(h * HD, (h + 1) * HD)
        for i, ref in enumerate((q_ref, g_ref, k_ref, v_ref)):
            out_ref[h, i * rows : (i + 1) * rows, :] = ref[:, cols]
        stats = jnp.where(row == 0, lse_high[j : j + 1], 0.0)
        stats = jnp.where(row == 1, lse_low[j : j + 1], stats)
        stats = jnp.where(row == 2, delta_high[h : h + 1], stats)
        stats = jnp.where(row == 3, delta_low[h : h + 1], stats)
        out_ref[h, 4 * rows : 4 * rows + 8, :] = stats.astype(BF16)


def placing(copy_ref, j):
    zh, xl = divmod(j, 2)
    shard = ((lax.axis_index("y") * 2 + zh) * 4 + lax.axis_index("xh") * 2 + xl) * 2 + lax.axis_index("c")
    copy = jnp.broadcast_to(copy_ref[pl.ds(shard, 1), :], (8, RUN)).astype(F32)
    upto = (iota((RUN, RUN), 0) <= iota((RUN, RUN), 1)).astype(BF16)
    count = contract(copy.astype(BF16), upto, 1, 0)
    index = iota((8, RUN), 1).astype(F32)
    place = jnp.where(copy > 0.5, HALF - 1.0 + count, index - count)
    place = jnp.broadcast_to(place[0:1], (RUN, RUN)).astype(jnp.int32)
    return (iota((RUN, RUN), 0) == place).astype(F32)


def sort_kernel(got_ref, copy_ref, qd_ref, kv_ref, kvn_ref):
    zl = lax.axis_index("zl")
    row = iota((8, RUN), 0)
    stats = []
    for j in range(RUNS):
        zh, xl = divmod(j, 2)
        one_hot = placing(copy_ref, j).astype(BF16)
        parts = [
            jnp.concatenate([got_ref[4 * z + j, 32 * i : 32 * i + 32, :] for z in range(4)], axis=0)
            for i in range(4)
        ]
        moved = contract(one_hot, jnp.concatenate(parts, axis=1), 1, 0).astype(BF16)
        qd_ref[256 * zh + 64 * xl : 256 * zh + 64 * xl + 64, :] = moved[:HALF, :256]
        qd_ref[256 * zh + 128 + 64 * xl : 256 * zh + 192 + 64 * xl, :] = moved[HALF:, :256]
        kvn_ref[128 * zh + 64 * xl : 128 * zh + 64 * xl + 64, :] = moved[:HALF, 256:]
        kv_ref[128 * zh + 64 * xl : 128 * zh + 64 * xl + 64, :] = moved[HALF:, 256:]
        lse = got_ref[4 * zl + j, 128:136, :].astype(F32)
        delta = jnp.concatenate(
            [got_ref[4 * z + j, 128:136, :].astype(F32)[:, :32] for z in range(4)], axis=1
        )
        both = jnp.where(row < 2, lse, delta)
        both = jnp.concatenate([both, jnp.zeros_like(both)], axis=0).astype(BF16)
        stats.append(contract(both, one_hot, 1, 1))
    halves = []
    for zh in range(2):
        a, b = stats[2 * zh], stats[2 * zh + 1]
        halves.append(
            jnp.concatenate([a[:8, :HALF], b[:8, :HALF], a[:8, HALF:], b[:8, HALF:]], axis=1)
        )
    qd_ref[512:528, :] = jnp.concatenate(halves, axis=0).astype(BF16)


def load_keys(pieces, k_all, kt_all, v_all):
    for m, ref in enumerate(pieces):
        rows = slice(256 * m, 256 * m + 256)
        k = ref[:, :HD]
        k_all[rows, :] = k
        v_all[rows, :] = ref[:, HD:]
        kt_all[:, rows] = k.astype(F32).T.astype(BF16)


def attend(ids_ref, qd_ref, other, masks, noisy, k_all, kt_all, v_all):
    y, xh = lax.axis_index("y"), lax.axis_index("xh")
    stats = qd_ref[512:528, :].astype(F32)
    lse = jnp.concatenate([stats[0:1] + stats[1:2], stats[8:9] + stats[9:10]], axis=1) * LOG2E
    delta = jnp.concatenate([stats[2:3] + stats[3:4], stats[10:11] + stats[11:12]], axis=1)
    lane = iota((1, 512), 1)
    clean, second = lane // 128 % 2 == 1, lane >= 256
    own_ids = [ids_ref[(y * 2 + zh) * 2 + (xh ^ other)] for zh in range(2)]
    limits = []
    for mask in masks:
        for zh in range(2):
            key_id = ids_ref[((y ^ mask) * 2 + zh) * 2 + xh]
            noisy_off, clean_off = (
                jnp.where(second, *(jnp.where(hit, 0.0, OFF) for hit in hits))
                for hits in ([key_id < i for i in own_ids[::-1]], [key_id <= i for i in own_ids[::-1]])
            )
            limits.append(lse + jnp.where(clean, clean_off, noisy_off))
    if noisy:
        limits.append(lse + jnp.where(clean | second, OFF, 0.0))
        limits.append(lse + jnp.where(clean | ~second, OFF, 0.0))
    q, g = qd_ref[:512, :HD], qd_ref[:512, HD:]
    scores = contract(k_all, q, 1, 1)
    weights = jnp.concatenate(
        [jnp.exp2(scores[128 * i : 128 * i + 128] * (SCALE * LOG2E) - row) for i, row in enumerate(limits)], axis=0
    )
    dweights = contract(v_all, g, 1, 1)
    dscores = (weights * (dweights - delta)).astype(BF16)
    dv = contract(weights.astype(BF16), g, 1, 0)
    dk = contract(dscores, q, 1, 0)
    return dk, dv, contract(kt_all, dscores, 1, 0).T * SCALE


def own_kernel(ids_ref, qd0, kv0, kvn_ref, dq_ref, dk_ref, dv_ref, k_all, kt_all, v_all):
    load_keys((kv0, kvn_ref), k_all, kt_all, v_all)
    dk_ref[...], dv_ref[...], dq_ref[...] = attend(
        ids_ref, qd0, 0, (0,), True, k_all[...], kt_all[...], v_all[...]
    )


def first_kernel(
    ids_ref, qd0, qd2, kv0, kv1, kv2, kv3, own_dq, own_dk, own_dv, dq_ref, dk_ref, dv_ref, k_all, kt_all, v_all
):
    load_keys((kv0, kv1, kv2, kv3), k_all, kt_all, v_all)
    far_dk, far_dv, dq_ref[1] = attend(ids_ref, qd2, 1, range(4), False, k_all[...], kt_all[...], v_all[...])
    dk, dv, dq = attend(
        ids_ref, qd0, 0, (1, 2, 3), False, k_all[256:, :], kt_all[:, 256:], v_all[256:, :]
    )
    dq_ref[0] = own_dq[...] + dq
    for total, own, near, far in ((dk_ref, own_dk, dk, far_dk), (dv_ref, own_dv, dv, far_dv)):
        total[:256, :] = own[:256, :] + far[:256]
        total[256:1024, :] = near + far[256:]
        total[1024:, :] = own[256:, :]


def second_kernel(
    ids_ref, qd1, qd3, kv0, kv1, kv2, kv3, kvn_ref, dk_ref, dv_ref,
    dq_ref, dkv0, dkv1, dkv2, dkv3, dkvn, k_all, kt_all, v_all,
):
    load_keys((kv0, kv1, kv2, kv3, kvn_ref), k_all, kt_all, v_all)
    near_dk, near_dv, dq = attend(ids_ref, qd1, 0, range(4), True, k_all[...], kt_all[...], v_all[...])
    dq_ref[0] = dq.astype(BF16)
    far_dk, far_dv, dq = attend(
        ids_ref, qd3, 1, range(4), False, k_all[:1024, :], kt_all[:, :1024], v_all[:1024, :]
    )
    dq_ref[1] = dq.astype(BF16)
    for m, ref in enumerate((dkv0, dkv1, dkv2, dkv3, dkvn)):
        rows = slice(256 * m, 256 * m + 256)
        dk, dv = dk_ref[rows, :] + near_dk[rows], dv_ref[rows, :] + near_dv[rows]
        if m < 4:
            dk, dv = dk + far_dk[rows], dv + far_dv[rows]
        ref[:, :HD] = (dk * SCALE).astype(ref.dtype)
        ref[:, HD:] = dv.astype(ref.dtype)


def add_kernel(keep_ref, got_ref, out_ref):
    out_ref[...] = (keep_ref[1] + got_ref[1].astype(F32)).astype(BF16)


def unsort_kernel(keep_ref, got_core, got_chip, dkv0, dkv1, dkv2, dkv3, dkvn_ref, copy_ref, out_ref):
    dq = (keep_ref[0] + got_core[0].astype(F32) + got_chip[...].astype(F32)).astype(BF16)
    dkv = (dkv0[...] + dkv1[...].astype(F32) + dkv2[...].astype(F32) + dkv3[...].astype(F32)).astype(BF16)
    for j in range(RUNS):
        zh, xl = divmod(j, 2)
        one_hot = placing(copy_ref, j).T.astype(BF16)
        at = 64 * xl
        queries = jnp.concatenate(
            [dq[256 * zh + at : 256 * zh + at + 64], dq[256 * zh + 128 + at : 256 * zh + 192 + at]], axis=0
        )
        keys = jnp.concatenate(
            [dkvn_ref[128 * zh + at : 128 * zh + at + 64, :], dkv[128 * zh + at : 128 * zh + at + 64]], axis=0
        )
        moved = contract(one_hot, jnp.concatenate([queries, keys], axis=1), 1, 0).astype(BF16)
        for z in range(4):
            for i in range(3):
                out_ref[4 * j + z, 32 * i : 32 * i + 32, :] = moved[32 * z : 32 * z + 32, HD * i : HD * (i + 1)]


def unpack_kernel(got_ref, dq_ref, dk_ref, dv_ref):
    rows = dq_ref.shape[0]
    for h in range(16):
        for i, ref in enumerate((dq_ref, dk_ref, dv_ref)):
            ref[:, h * HD : (h + 1) * HD] = got_ref[4 * (h % 4) + h // 4, i * rows : (i + 1) * rows, :]


def swap(x, mask):
    return lax.ppermute(x, QUERY_AXES, [(i, i ^ mask) for i in range(4)])


def swap_y(x, mask):
    return lax.ppermute(x, "y", [(i, i ^ mask) for i in range(4)])


def shape(dims, dtype=BF16):
    return jax.ShapeDtypeStruct(dims, dtype)


def per_device(query_in, key_in, value_in, saved_out, grad_out, saved_lse, row_block, row_copy):
    copies = row_copy.reshape(-1, RUN)
    ids = row_block[:: 4 * RUN]
    rows = query_in.shape[0]
    arrays = (query_in, key_in, value_in, saved_out, grad_out, saved_lse.T)
    packed = call(
        pack_kernel,
        shape((16, 4 * rows + 8, HD)),
        tuple(pltpu.with_memory_space_constraint(x, pltpu.HBM) for x in arrays),
        hbm=range(6),
        scratch=[pltpu.VMEM(query_in.shape, BF16)] * 5 + [pltpu.VMEM((4, 128), F32), pltpu.SemaphoreType.DMA((6,))],
    )
    got = lax.all_to_all(packed, HEAD_AXES, 0, 0, tiled=True)
    qd, kv, kvn = call(
        sort_kernel, (shape((528, 256)), shape((256, 256)), shape((256, 256))), (got, copies)
    )
    qd2 = swap(qd, 2)
    kv3, kv2, kv1 = (swap_y(kv, m) for m in (3, 2, 1))
    def scratch(count):
        return pltpu.VMEM((count, HD), BF16), pltpu.VMEM((HD, count), BF16), pltpu.VMEM((count, HD), BF16)

    part = shape((512, HD), F32)
    own = call(own_kernel, (part,) * 3, (ids, qd, kv, kvn), smem=(0,), scratch=scratch(512))
    qd2, kv3, kv2, kv1, ids, qd, *own = lax.optimization_barrier((qd2, kv3, kv2, kv1, ids, qd, *own))
    qd1 = swap(qd, 1)
    qd3 = swap(qd2, 1)
    keys = (kv, kv1, kv2, kv3)
    total = shape((1280, HD), F32)
    dq_keep, dk, dv = call(
        first_kernel,
        (shape((2, 512, HD), F32), total, total),
        (ids, qd, qd2, *keys, *own),
        smem=(0,),
        scratch=scratch(1024),
    )
    dq_send, *dkvs, dkvn = call(
        second_kernel,
        (shape((2, 512, HD)), shape((256, 256), F32)) + (shape((256, 256)),) * 4,
        (ids, qd1, qd3, *keys, kvn, dk, dv),
        smem=(0,),
        scratch=scratch(1280),
    )
    dq_core = swap(dq_send, 1)
    for m in (2, 1, 3):
        dkvs[m] = swap_y(dkvs[m], m)
    dq_chip = swap(call(add_kernel, shape((512, HD)), (dq_keep, dq_core)), 2)
    back = call(unsort_kernel, shape((16, 3 * rows, HD)), (dq_keep, dq_core, dq_chip, dkvs[0], dkvs[3], dkvs[2], dkvs[1], dkvn, copies))
    back = lax.all_to_all(back, BACK_AXES, 0, 0, tiled=True)
    return call(unpack_kernel, (shape((rows, 16 * HD)),) * 3, (back,))


def solution(mesh):
    fine = Mesh(mesh.devices.reshape(SIZES), AXES)
    whole = P(AXES, None)
    return jax.shard_map(
        per_device,
        mesh=fine,
        in_specs=(whole, whole, whole, whole, whole, P(AXES[:5], AXES[5]), P(), P()),
        out_specs=(whole, whole, whole),
        check_vma=False,
    )
```

```python
import jax
import jax.numpy as jnp
from jax import lax
from jax.experimental import pallas as pl
from jax.experimental.pallas import tpu as pltpu
from jax.sharding import Mesh
from jax.sharding import PartitionSpec as P

HD = 128
RUN = 128
HALF = RUN // 2
AXES = ("y", "zh", "xh", "xl", "c", "zl")
SIZES = (4, 2, 2, 2, 2, 4)
HEAD_AXES = ("zl", "zh", "xl")
BACK_AXES = ("zh", "xl", "zl")
QUERY_AXES = ("xh", "c")
RUNS = 4
SCALE = HD**-0.5
LOG2E = 1.4426950408889634
OFF = 1e30
F32 = jnp.float32
BF16 = jnp.bfloat16
VMEM = pl.BlockSpec(memory_space=pltpu.VMEM)
HBM = pl.BlockSpec(memory_space=pltpu.HBM)
SMEM = pl.BlockSpec(memory_space=pltpu.SMEM)


def iota(shape, axis):
    return lax.broadcasted_iota(jnp.int32, shape, axis)


def split_two(x):
    high = x.astype(BF16).astype(F32)
    return high, x - high


def contract(a, b, dim_a, dim_b):
    return lax.dot_general(a, b, (((dim_a,), (dim_b,)), ((), ())), preferred_element_type=F32)


def call(body, out_shape, args, smem=(), hbm=(), scratch=(), limit=32 << 20, cost=None):
    return pl.pallas_call(
        body,
        out_shape=out_shape,
        in_specs=[SMEM if i in smem else HBM if i in hbm else VMEM for i in range(len(args))],
        out_specs=jax.tree.map(lambda _: VMEM, out_shape),
        scratch_shapes=list(scratch),
        compiler_params=pltpu.CompilerParams(vmem_limit_bytes=limit),
        cost_estimate=cost,
    )(*args)


def pack_kernel(q_in, k_in, v_in, o_in, g_in, lse_in, out_ref, q_ref, k_ref, v_ref, o_ref, g_ref, lse_ref, sems):
    pairs = ((g_in, g_ref), (o_in, o_ref), (lse_in, lse_ref), (q_in, q_ref), (k_in, k_ref), (v_in, v_ref))
    copies = [pltpu.make_async_copy(a, b, sems.at[i]) for i, (a, b) in enumerate(pairs)]
    for copy in copies:
        copy.start()
    rows = q_ref.shape[0]
    for copy in copies[:3]:
        copy.wait()
    lane = iota((rows, 128), 1)
    delta = jnp.zeros((rows, 128), F32)
    for h in range(16):
        cols = slice(h * HD, (h + 1) * HD)
        term = g_ref[:, cols].astype(F32) * o_ref[:, cols].astype(F32)
        delta = jnp.where(lane == h, jnp.sum(term, axis=1, keepdims=True), delta)
    delta = jnp.concatenate([delta, jnp.zeros((128 - rows, 128), F32)], axis=0).T
    delta_high, delta_low = split_two(delta)
    lse_high, lse_low = split_two(lse_ref[...])
    row = iota((8, 128), 0)
    for copy in copies[3:]:
        copy.wait()
    for h in range(16):
        j = h % 4
        cols = slice(h * HD, (h + 1) * HD)
        for i, ref in enumerate((q_ref, g_ref, k_ref, v_ref)):
            out_ref[h, i * rows : (i + 1) * rows, :] = ref[:, cols]
        stats = jnp.where(row == 0, lse_high[j : j + 1], 0.0)
        stats = jnp.where(row == 1, lse_low[j : j + 1], stats)
        stats = jnp.where(row == 2, delta_high[h : h + 1], stats)
        stats = jnp.where(row == 3, delta_low[h : h + 1], stats)
        out_ref[h, 4 * rows : 4 * rows + 8, :] = stats.astype(BF16)


def placing(copy_ref, j):
    zh, xl = divmod(j, 2)
    shard = ((lax.axis_index("y") * 2 + zh) * 4 + lax.axis_index("xh") * 2 + xl) * 2 + lax.axis_index("c")
    copy = jnp.broadcast_to(copy_ref[pl.ds(shard, 1), :], (8, RUN)).astype(F32)
    upto = (iota((RUN, RUN), 0) <= iota((RUN, RUN), 1)).astype(BF16)
    count = contract(copy.astype(BF16), upto, 1, 0)
    index = iota((8, RUN), 1).astype(F32)
    place = jnp.where(copy > 0.5, HALF - 1.0 + count, index - count)
    place = jnp.broadcast_to(place[0:1], (RUN, RUN)).astype(jnp.int32)
    return (iota((RUN, RUN), 0) == place).astype(F32)


def sort_kernel(got_ref, copy_ref, qd_ref, kv_ref, kvn_ref):
    zl = lax.axis_index("zl")
    row = iota((8, RUN), 0)
    stats = []
    for j in range(RUNS):
        zh, xl = divmod(j, 2)
        one_hot = placing(copy_ref, j).astype(BF16)
        parts = [
            jnp.concatenate([got_ref[4 * z + j, 32 * i : 32 * i + 32, :] for z in range(4)], axis=0)
            for i in range(4)
        ]
        moved = contract(one_hot, jnp.concatenate(parts, axis=1), 1, 0).astype(BF16)
        qd_ref[256 * zh + 64 * xl : 256 * zh + 64 * xl + 64, :] = moved[:HALF, :256]
        qd_ref[256 * zh + 128 + 64 * xl : 256 * zh + 192 + 64 * xl, :] = moved[HALF:, :256]
        kvn_ref[128 * zh + 64 * xl : 128 * zh + 64 * xl + 64, :] = moved[:HALF, 256:]
        kv_ref[128 * zh + 64 * xl : 128 * zh + 64 * xl + 64, :] = moved[HALF:, 256:]
        lse = got_ref[4 * zl + j, 128:136, :].astype(F32)
        delta = jnp.concatenate(
            [got_ref[4 * z + j, 128:136, :].astype(F32)[:, :32] for z in range(4)], axis=1
        )
        both = jnp.where(row < 2, lse, delta)
        both = jnp.concatenate([both, jnp.zeros_like(both)], axis=0).astype(BF16)
        stats.append(contract(both, one_hot, 1, 1))
    halves = []
    for zh in range(2):
        a, b = stats[2 * zh], stats[2 * zh + 1]
        halves.append(
            jnp.concatenate([a[:8, :HALF], b[:8, :HALF], a[:8, HALF:], b[:8, HALF:]], axis=1)
        )
    qd_ref[512:528, :] = jnp.concatenate(halves, axis=0).astype(BF16)


def load_keys(pieces, k_all, kt_all, v_all):
    for m, ref in enumerate(pieces):
        rows = slice(256 * m, 256 * m + 256)
        k = ref[:, :HD]
        k_all[rows, :] = k
        v_all[rows, :] = ref[:, HD:]
        kt_all[:, rows] = k.astype(F32).T.astype(BF16)


def attend(ids_ref, qd_ref, other, masks, noisy, k_all, kt_all, v_all):
    y, xh = lax.axis_index("y"), lax.axis_index("xh")
    stats = qd_ref[512:528, :].astype(F32)
    lse = jnp.concatenate([stats[0:1] + stats[1:2], stats[8:9] + stats[9:10]], axis=1) * LOG2E
    delta = jnp.concatenate([stats[2:3] + stats[3:4], stats[10:11] + stats[11:12]], axis=1)
    lane = iota((1, 512), 1)
    clean, second = lane // 128 % 2 == 1, lane >= 256
    own_ids = [ids_ref[(y * 2 + zh) * 2 + (xh ^ other)] for zh in range(2)]
    limits = []
    for mask in masks:
        for zh in range(2):
            key_id = ids_ref[((y ^ mask) * 2 + zh) * 2 + xh]
            noisy_off, clean_off = (
                jnp.where(second, *(jnp.where(hit, 0.0, OFF) for hit in hits))
                for hits in ([key_id < i for i in own_ids[::-1]], [key_id <= i for i in own_ids[::-1]])
            )
            limits.append(lse + jnp.where(clean, clean_off, noisy_off))
    if noisy:
        limits.append(lse + jnp.where(clean | second, OFF, 0.0))
        limits.append(lse + jnp.where(clean | ~second, OFF, 0.0))
    q, g = qd_ref[:512, :HD], qd_ref[:512, HD:]
    scores = contract(k_all, q, 1, 1)
    weights = jnp.concatenate(
        [jnp.exp2(scores[128 * i : 128 * i + 128] * (SCALE * LOG2E) - row) for i, row in enumerate(limits)], axis=0
    )
    dweights = contract(v_all, g, 1, 1)
    dscores = (weights * (dweights - delta)).astype(BF16)
    dv = contract(weights.astype(BF16), g, 1, 0)
    dk = contract(dscores, q, 1, 0)
    return dk, dv, contract(kt_all, dscores, 1, 0).T * SCALE


def own_kernel(ids_ref, qd0, kv0, kvn_ref, dq_ref, dk_ref, dv_ref, k_all, kt_all, v_all):
    load_keys((kv0, kvn_ref), k_all, kt_all, v_all)
    dk_ref[...], dv_ref[...], dq_ref[...] = attend(
        ids_ref, qd0, 0, (0,), True, k_all[...], kt_all[...], v_all[...]
    )


def first_kernel(
    ids_ref, qd0, qd2, kv0, kv1, kv2, kv3, own_dq, own_dk, own_dv, dq_ref, dk_ref, dv_ref, k_all, kt_all, v_all
):
    load_keys((kv0, kv1, kv2, kv3), k_all, kt_all, v_all)
    far_dk, far_dv, dq_ref[1] = attend(ids_ref, qd2, 1, range(4), False, k_all[...], kt_all[...], v_all[...])
    dk, dv, dq = attend(
        ids_ref, qd0, 0, (1, 2, 3), False, k_all[256:, :], kt_all[:, 256:], v_all[256:, :]
    )
    dq_ref[0] = own_dq[...] + dq
    for total, own, near, far in ((dk_ref, own_dk, dk, far_dk), (dv_ref, own_dv, dv, far_dv)):
        total[:256, :] = own[:256, :] + far[:256]
        total[256:1024, :] = near + far[256:]
        total[1024:, :] = own[256:, :]


def second_kernel(
    ids_ref, qd1, qd3, kv0, kv1, kv2, kv3, kvn_ref, dk_ref, dv_ref,
    dq_ref, dkv0, dkv1, dkv2, dkv3, dkvn, k_all, kt_all, v_all,
):
    load_keys((kv0, kv1, kv2, kv3, kvn_ref), k_all, kt_all, v_all)
    near_dk, near_dv, dq = attend(ids_ref, qd1, 0, range(4), True, k_all[...], kt_all[...], v_all[...])
    dq_ref[0] = dq.astype(BF16)
    far_dk, far_dv, dq = attend(
        ids_ref, qd3, 1, range(4), False, k_all[:1024, :], kt_all[:, :1024], v_all[:1024, :]
    )
    dq_ref[1] = dq.astype(BF16)
    for m, ref in enumerate((dkv0, dkv1, dkv2, dkv3, dkvn)):
        rows = slice(256 * m, 256 * m + 256)
        dk, dv = dk_ref[rows, :] + near_dk[rows], dv_ref[rows, :] + near_dv[rows]
        if m < 4:
            dk, dv = dk + far_dk[rows], dv + far_dv[rows]
        ref[:, :HD] = (dk * SCALE).astype(ref.dtype)
        ref[:, HD:] = dv.astype(ref.dtype)


def add_kernel(keep_ref, got_ref, send_ref, sum_ref):
    send_ref[...] = (keep_ref[1] + got_ref[1].astype(F32)).astype(BF16)
    sum_ref[...] = keep_ref[0] + got_ref[0].astype(F32)


def prepare_kernel(dkvn_ref, copy_ref, one_hot_ref, noisy_ref):
    for j in range(RUNS):
        one_hot = placing(copy_ref, j).T.astype(BF16)
        one_hot_ref[j] = one_hot
        rows = dkvn_ref[64 * j : 64 * j + 64, :]
        noisy_ref[j] = contract(one_hot, jnp.concatenate([rows, jnp.zeros_like(rows)], axis=0), 1, 0).astype(BF16)


def unsort_kernel(sum_ref, got_chip, dkv0, dkv1, dkv2, dkv3, one_hot_ref, noisy_ref, out_ref):
    dq = (sum_ref[...] + got_chip[...].astype(F32)).astype(BF16)
    dkv = (dkv0[...] + dkv1[...].astype(F32) + dkv2[...].astype(F32) + dkv3[...].astype(F32)).astype(BF16)
    for j in range(RUNS):
        zh, xl = divmod(j, 2)
        at = 64 * xl
        queries = jnp.concatenate(
            [dq[256 * zh + at : 256 * zh + at + 64], dq[256 * zh + 128 + at : 256 * zh + 192 + at]], axis=0
        )
        rows = dkv[64 * j : 64 * j + 64]
        keys = jnp.concatenate([jnp.zeros_like(rows), rows], axis=0)
        moved = contract(one_hot_ref[j], jnp.concatenate([queries, keys], axis=1), 1, 0)
        moved_keys = (moved[:, HD:] + noisy_ref[j].astype(F32)).astype(BF16)
        moved = jnp.concatenate([moved[:, :HD].astype(BF16), moved_keys], axis=1)
        for z in range(4):
            for i in range(3):
                out_ref[4 * j + z, 32 * i : 32 * i + 32, :] = moved[32 * z : 32 * z + 32, HD * i : HD * (i + 1)]


def unpack_kernel(got_ref, dq_ref, dk_ref, dv_ref):
    rows = dq_ref.shape[0]
    for h in range(16):
        for i, ref in enumerate((dq_ref, dk_ref, dv_ref)):
            ref[:, h * HD : (h + 1) * HD] = got_ref[4 * (h % 4) + h // 4, i * rows : (i + 1) * rows, :]


def swap(x, mask):
    return lax.ppermute(x, QUERY_AXES, [(i, i ^ mask) for i in range(4)])


def swap_y(x, mask):
    return lax.ppermute(x, "y", [(i, i ^ mask) for i in range(4)])


def shape(dims, dtype=BF16):
    return jax.ShapeDtypeStruct(dims, dtype)


def per_device(query_in, key_in, value_in, saved_out, grad_out, saved_lse, row_block, row_copy):
    copies = row_copy.reshape(-1, RUN)
    ids = row_block[:: 4 * RUN]
    rows = query_in.shape[0]
    arrays = (query_in, key_in, value_in, saved_out, grad_out, saved_lse.T)
    packed = call(
        pack_kernel,
        shape((16, 4 * rows + 8, HD)),
        tuple(pltpu.with_memory_space_constraint(x, pltpu.HBM) for x in arrays),
        hbm=range(6),
        scratch=[pltpu.VMEM(query_in.shape, BF16)] * 5 + [pltpu.VMEM((4, 128), F32), pltpu.SemaphoreType.DMA((6,))],
    )
    got = lax.all_to_all(packed, HEAD_AXES, 0, 0, tiled=True)
    qd, kv, kvn = call(
        sort_kernel, (shape((528, 256)), shape((256, 256)), shape((256, 256))), (got, copies)
    )
    qd2 = swap(qd, 2)
    kv3, kv2, kv1 = (swap_y(kv, m) for m in (3, 2, 1))
    def scratch(count):
        return pltpu.VMEM((count, HD), BF16), pltpu.VMEM((HD, count), BF16), pltpu.VMEM((count, HD), BF16)

    part = shape((512, HD), F32)
    own = call(own_kernel, (part,) * 3, (ids, qd, kv, kvn), smem=(0,), scratch=scratch(512))
    qd2, kv3, kv2, kv1, ids, qd, *own = lax.optimization_barrier((qd2, kv3, kv2, kv1, ids, qd, *own))
    qd1 = swap(qd, 1)
    qd3 = swap(qd2, 1)
    keys = (kv, kv1, kv2, kv3)
    total = shape((1280, HD), F32)
    dq_keep, dk, dv = call(
        first_kernel,
        (shape((2, 512, HD), F32), total, total),
        (ids, qd, qd2, *keys, *own),
        smem=(0,),
        scratch=scratch(1024),
    )
    dq_send, *dkvs, dkvn = call(
        second_kernel,
        (shape((2, 512, HD)), shape((256, 256), F32)) + (shape((256, 256)),) * 4,
        (ids, qd1, qd3, *keys, kvn, dk, dv),
        smem=(0,),
        scratch=scratch(1280),
    )
    dq_core = swap(dq_send, 1)
    for m in (2, 1, 3):
        dkvs[m] = swap_y(dkvs[m], m)
    half, dq_sum = call(add_kernel, (shape((512, HD)), shape((512, HD), F32)), (dq_keep, dq_core))
    one_hot, noisy = call(
        prepare_kernel, (shape((RUNS, RUN, RUN)), shape((RUNS, RUN, 256))), (dkvn, copies)
    )
    back = call(
        unsort_kernel,
        shape((16, 3 * rows, HD)),
        (dq_sum, swap(half, 2), dkvs[0], dkvs[3], dkvs[2], dkvs[1], one_hot, noisy),
    )
    back = lax.all_to_all(back, BACK_AXES, 0, 0, tiled=True)
    return call(unpack_kernel, (shape((rows, 16 * HD)),) * 3, (back,))


def solution(mesh):
    fine = Mesh(mesh.devices.reshape(SIZES), AXES)
    whole = P(AXES, None)
    return jax.shard_map(
        per_device,
        mesh=fine,
        in_specs=(whole, whole, whole, whole, whole, P(AXES[:5], AXES[5]), P(), P()),
        out_specs=(whole, whole, whole),
        check_vma=False,
    )
```

```python
import jax
import jax.numpy as jnp
from jax import lax
from jax.experimental import pallas as pl
from jax.experimental.pallas import tpu as pltpu
from jax.sharding import Mesh
from jax.sharding import PartitionSpec as P

HD = 128
RUN = 128
HALF = RUN // 2
AXES = ("y", "zh", "xh", "xl", "c", "zl")
SIZES = (4, 2, 2, 2, 2, 4)
HEAD_AXES = ("zl", "zh", "xl")
BACK_AXES = ("zh", "xl", "zl")
QUERY_AXES = ("xh", "c")
RUNS = 4
SCALE = HD**-0.5
LOG2E = 1.4426950408889634
OFF = 1e30
F32 = jnp.float32
BF16 = jnp.bfloat16
VMEM = pl.BlockSpec(memory_space=pltpu.VMEM)
HBM = pl.BlockSpec(memory_space=pltpu.HBM)
SMEM = pl.BlockSpec(memory_space=pltpu.SMEM)


def iota(shape, axis):
    return lax.broadcasted_iota(jnp.int32, shape, axis)


def split_two(x):
    high = x.astype(BF16).astype(F32)
    return high, x - high


def contract(a, b, dim_a, dim_b):
    return lax.dot_general(a, b, (((dim_a,), (dim_b,)), ((), ())), preferred_element_type=F32)


def call(body, out_shape, args, smem=(), hbm=(), scratch=(), limit=32 << 20, cost=None):
    return pl.pallas_call(
        body,
        out_shape=out_shape,
        in_specs=[SMEM if i in smem else HBM if i in hbm else VMEM for i in range(len(args))],
        out_specs=jax.tree.map(lambda _: VMEM, out_shape),
        scratch_shapes=list(scratch),
        compiler_params=pltpu.CompilerParams(vmem_limit_bytes=limit),
        cost_estimate=cost,
    )(*args)


def pack_kernel(q_in, k_in, v_in, o_in, g_in, lse_in, out_ref, q_ref, k_ref, v_ref, o_ref, g_ref, lse_ref, sems):
    pairs = ((g_in, g_ref), (o_in, o_ref), (lse_in, lse_ref), (q_in, q_ref), (k_in, k_ref), (v_in, v_ref))
    copies = [pltpu.make_async_copy(a, b, sems.at[i]) for i, (a, b) in enumerate(pairs)]
    for copy in copies:
        copy.start()
    rows = q_ref.shape[0]
    for copy in copies[:3]:
        copy.wait()
    lane = iota((rows, 128), 1)
    delta = jnp.zeros((rows, 128), F32)
    for h in range(16):
        cols = slice(h * HD, (h + 1) * HD)
        term = g_ref[:, cols].astype(F32) * o_ref[:, cols].astype(F32)
        delta = jnp.where(lane == h, jnp.sum(term, axis=1, keepdims=True), delta)
    delta = jnp.concatenate([delta, jnp.zeros((128 - rows, 128), F32)], axis=0).T
    delta_high, delta_low = split_two(delta)
    lse_high, lse_low = split_two(lse_ref[...])
    row = iota((16, 128), 0)
    for copy in copies[3:]:
        copy.wait()
    for h in range(16):
        j = h % 4
        cols = slice(h * HD, (h + 1) * HD)
        for i, ref in enumerate((q_ref, g_ref, k_ref, v_ref)):
            out_ref[h, i * rows : (i + 1) * rows, :] = ref[:, cols]
        stats = jnp.where(row == 0, lse_high[j : j + 1], 0.0)
        stats = jnp.where(row == 1, lse_low[j : j + 1], stats)
        stats = jnp.where(row == 2, delta_high[h : h + 1], stats)
        stats = jnp.where(row == 3, delta_low[h : h + 1], stats)
        out_ref[h, 4 * rows : 4 * rows + 16, :] = stats.astype(BF16)


def placing(copy_ref, j):
    zh, xl = divmod(j, 2)
    shard = ((lax.axis_index("y") * 2 + zh) * 4 + lax.axis_index("xh") * 2 + xl) * 2 + lax.axis_index("c")
    copy = jnp.broadcast_to(copy_ref[pl.ds(shard, 1), :], (8, RUN)).astype(F32)
    upto = (iota((RUN, RUN), 0) <= iota((RUN, RUN), 1)).astype(BF16)
    count = contract(copy.astype(BF16), upto, 1, 0)
    index = iota((8, RUN), 1).astype(F32)
    place = jnp.where(copy > 0.5, HALF - 1.0 + count, index - count)
    place = jnp.broadcast_to(place[0:1], (RUN, RUN)).astype(jnp.int32)
    return (iota((RUN, RUN), 0) == place).astype(F32)


def sort_kernel(got_ref, copy_ref, qd_ref, kv_ref, kvn_ref):
    zl = lax.axis_index("zl")
    row = iota((16, RUN), 0)
    stats = []
    for j in range(RUNS):
        zh, xl = divmod(j, 2)
        one_hot = placing(copy_ref, j).astype(BF16)
        parts = [
            jnp.concatenate([got_ref[4 * z + j, 32 * i : 32 * i + 32, :] for z in range(4)], axis=0)
            for i in range(4)
        ]
        moved = contract(one_hot, jnp.concatenate(parts, axis=1), 1, 0).astype(BF16)
        qd_ref[256 * zh + 64 * xl : 256 * zh + 64 * xl + 64, :] = moved[:HALF, :256]
        qd_ref[256 * zh + 128 + 64 * xl : 256 * zh + 192 + 64 * xl, :] = moved[HALF:, :256]
        kvn_ref[128 * zh + 64 * xl : 128 * zh + 64 * xl + 64, :] = moved[:HALF, 256:]
        kv_ref[128 * zh + 64 * xl : 128 * zh + 64 * xl + 64, :] = moved[HALF:, 256:]
        lse = got_ref[4 * zl + j, 128:144, :].astype(F32)
        delta = jnp.concatenate(
            [got_ref[4 * z + j, 128:144, :].astype(F32)[:, :32] for z in range(4)], axis=1
        )
        both = jnp.where(row < 2, lse, delta).astype(BF16)
        stats.append(contract(both, one_hot, 1, 1))
    halves = []
    for zh in range(2):
        a, b = stats[2 * zh], stats[2 * zh + 1]
        halves.append(
            jnp.concatenate([a[:8, :HALF], b[:8, :HALF], a[:8, HALF:], b[:8, HALF:]], axis=1)
        )
    qd_ref[512:528, :] = jnp.concatenate(halves, axis=0).astype(BF16)


def load_keys(pieces, k_all, kt_all, v_all):
    for m, ref in enumerate(pieces):
        rows = slice(256 * m, 256 * m + 256)
        k = ref[:, :HD]
        k_all[rows, :] = k
        v_all[rows, :] = ref[:, HD:]
        kt_all[:, rows] = k.astype(F32).T.astype(BF16)


def attend(ids_ref, qd_ref, other, masks, noisy, k_all, kt_all, v_all):
    y, xh = lax.axis_index("y"), lax.axis_index("xh")
    stats = qd_ref[512:528, :].astype(F32)
    lse = jnp.concatenate([stats[0:1] + stats[1:2], stats[8:9] + stats[9:10]], axis=1) * LOG2E
    delta = jnp.concatenate([stats[2:3] + stats[3:4], stats[10:11] + stats[11:12]], axis=1)
    lane = iota((1, 512), 1)
    clean, second = lane // 128 % 2 == 1, lane >= 256
    own_ids = [ids_ref[(y * 2 + zh) * 2 + (xh ^ other)] for zh in range(2)]
    limits = []
    for mask in masks:
        for zh in range(2):
            key_id = ids_ref[((y ^ mask) * 2 + zh) * 2 + xh]
            noisy_off, clean_off = (
                jnp.where(second, *(jnp.where(hit, 0.0, OFF) for hit in hits))
                for hits in ([key_id < i for i in own_ids[::-1]], [key_id <= i for i in own_ids[::-1]])
            )
            limits.append(lse + jnp.where(clean, clean_off, noisy_off))
    if noisy:
        limits.append(lse + jnp.where(clean | second, OFF, 0.0))
        limits.append(lse + jnp.where(clean | ~second, OFF, 0.0))
    q, g = qd_ref[:512, :HD], qd_ref[:512, HD:]
    scores = contract(k_all, q, 1, 1)
    weights = jnp.concatenate(
        [jnp.exp2(scores[128 * i : 128 * i + 128] * (SCALE * LOG2E) - row) for i, row in enumerate(limits)], axis=0
    )
    dweights = contract(v_all, g, 1, 1)
    dscores = (weights * (dweights - delta)).astype(BF16)
    dv = contract(weights.astype(BF16), g, 1, 0)
    dk = contract(dscores, q, 1, 0)
    return dk, dv, contract(kt_all, dscores, 1, 0).T * SCALE


def own_kernel(ids_ref, qd0, kv0, kvn_ref, dq_ref, dk_ref, dv_ref, k_all, kt_all, v_all):
    load_keys((kv0, kvn_ref), k_all, kt_all, v_all)
    dk_ref[...], dv_ref[...], dq_ref[...] = attend(
        ids_ref, qd0, 0, (0,), True, k_all[...], kt_all[...], v_all[...]
    )


def first_kernel(
    ids_ref, qd0, qd2, kv0, kv1, kv2, kv3, own_dq, own_dk, own_dv, dq_ref, dk_ref, dv_ref, k_all, kt_all, v_all
):
    load_keys((kv0, kv1, kv2, kv3), k_all, kt_all, v_all)
    far_dk, far_dv, dq_ref[1] = attend(ids_ref, qd2, 1, range(4), False, k_all[...], kt_all[...], v_all[...])
    dk, dv, dq = attend(
        ids_ref, qd0, 0, (1, 2, 3), False, k_all[256:, :], kt_all[:, 256:], v_all[256:, :]
    )
    dq_ref[0] = own_dq[...] + dq
    for total, own, near, far in ((dk_ref, own_dk, dk, far_dk), (dv_ref, own_dv, dv, far_dv)):
        total[:256, :] = own[:256, :] + far[:256]
        total[256:1024, :] = near + far[256:]
        total[1024:, :] = own[256:, :]


def second_kernel(
    ids_ref, qd1, qd3, kv0, kv1, kv2, kv3, kvn_ref, dk_ref, dv_ref,
    dq_ref, dkv0, dkv1, dkv2, dkv3, dkvn, k_all, kt_all, v_all,
):
    load_keys((kv0, kv1, kv2, kv3, kvn_ref), k_all, kt_all, v_all)
    near_dk, near_dv, dq = attend(ids_ref, qd1, 0, range(4), True, k_all[...], kt_all[...], v_all[...])
    dq_ref[0] = dq.astype(BF16)
    far_dk, far_dv, dq = attend(
        ids_ref, qd3, 1, range(4), False, k_all[:1024, :], kt_all[:, :1024], v_all[:1024, :]
    )
    dq_ref[1] = dq.astype(BF16)
    for m, ref in enumerate((dkv0, dkv1, dkv2, dkv3, dkvn)):
        rows = slice(256 * m, 256 * m + 256)
        dk, dv = dk_ref[rows, :] + near_dk[rows], dv_ref[rows, :] + near_dv[rows]
        if m < 4:
            dk, dv = dk + far_dk[rows], dv + far_dv[rows]
        ref[:, :HD] = (dk * SCALE).astype(ref.dtype)
        ref[:, HD:] = dv.astype(ref.dtype)


def add_kernel(keep_ref, got_ref, send_ref, sum_ref):
    send_ref[...] = (keep_ref[1] + got_ref[1].astype(F32)).astype(BF16)
    sum_ref[...] = keep_ref[0] + got_ref[0].astype(F32)


def prepare_kernel(dkvn_ref, copy_ref, one_hot_ref, noisy_ref):
    for j in range(RUNS):
        one_hot = placing(copy_ref, j).T.astype(BF16)
        one_hot_ref[j] = one_hot
        rows = dkvn_ref[64 * j : 64 * j + 64, :]
        noisy_ref[j] = contract(one_hot, jnp.concatenate([rows, jnp.zeros_like(rows)], axis=0), 1, 0).astype(BF16)


def unsort_kernel(sum_ref, got_chip, dkv0, dkv1, dkv2, dkv3, one_hot_ref, noisy_ref, out_ref):
    dq = (sum_ref[...] + got_chip[...].astype(F32)).astype(BF16)
    dkv = (dkv0[...] + dkv1[...].astype(F32) + dkv2[...].astype(F32) + dkv3[...].astype(F32)).astype(BF16)
    for j in range(RUNS):
        zh, xl = divmod(j, 2)
        at = 64 * xl
        queries = jnp.concatenate(
            [dq[256 * zh + at : 256 * zh + at + 64], dq[256 * zh + 128 + at : 256 * zh + 192 + at]], axis=0
        )
        rows = dkv[64 * j : 64 * j + 64]
        keys = jnp.concatenate([jnp.zeros_like(rows), rows], axis=0)
        moved = contract(one_hot_ref[j], jnp.concatenate([queries, keys], axis=1), 1, 0)
        moved_keys = (moved[:, HD:] + noisy_ref[j].astype(F32)).astype(BF16)
        moved = jnp.concatenate([moved[:, :HD].astype(BF16), moved_keys], axis=1)
        for z in range(4):
            for i in range(3):
                out_ref[4 * j + z, 32 * i : 32 * i + 32, :] = moved[32 * z : 32 * z + 32, HD * i : HD * (i + 1)]


def unpack_kernel(got_ref, dq_ref, dk_ref, dv_ref):
    rows = dq_ref.shape[0]
    for h in range(16):
        for i, ref in enumerate((dq_ref, dk_ref, dv_ref)):
            ref[:, h * HD : (h + 1) * HD] = got_ref[4 * (h % 4) + h // 4, i * rows : (i + 1) * rows, :]


def swap(x, mask):
    return lax.ppermute(x, QUERY_AXES, [(i, i ^ mask) for i in range(4)])


def swap_y(x, mask):
    return lax.ppermute(x, "y", [(i, i ^ mask) for i in range(4)])


def shape(dims, dtype=BF16):
    return jax.ShapeDtypeStruct(dims, dtype)


def per_device(query_in, key_in, value_in, saved_out, grad_out, saved_lse, row_block, row_copy):
    copies = row_copy.reshape(-1, RUN)
    ids = row_block[:: 4 * RUN]
    rows = query_in.shape[0]
    arrays = (query_in, key_in, value_in, saved_out, grad_out, saved_lse.T)
    packed = call(
        pack_kernel,
        shape((16, 4 * rows + 16, HD)),
        tuple(pltpu.with_memory_space_constraint(x, pltpu.HBM) for x in arrays),
        hbm=range(6),
        scratch=[pltpu.VMEM(query_in.shape, BF16)] * 5 + [pltpu.VMEM((4, 128), F32), pltpu.SemaphoreType.DMA((6,))],
    )
    got = lax.all_to_all(packed, HEAD_AXES, 0, 0, tiled=True)
    qd, kv, kvn = call(
        sort_kernel, (shape((528, 256)), shape((256, 256)), shape((256, 256))), (got, copies)
    )
    qd2 = swap(qd, 2)
    kv3, kv2, kv1 = (swap_y(kv, m) for m in (3, 2, 1))
    def scratch(count):
        return pltpu.VMEM((count, HD), BF16), pltpu.VMEM((HD, count), BF16), pltpu.VMEM((count, HD), BF16)

    part = shape((512, HD), F32)
    own = call(own_kernel, (part,) * 3, (ids, qd, kv, kvn), smem=(0,), scratch=scratch(512))
    qd2, kv3, kv2, kv1, ids, qd, *own = lax.optimization_barrier((qd2, kv3, kv2, kv1, ids, qd, *own))
    qd1 = swap(qd, 1)
    qd3 = swap(qd2, 1)
    keys = (kv, kv1, kv2, kv3)
    total = shape((1280, HD), F32)
    dq_keep, dk, dv = call(
        first_kernel,
        (shape((2, 512, HD), F32), total, total),
        (ids, qd, qd2, *keys, *own),
        smem=(0,),
        scratch=scratch(1024),
    )
    dq_send, *dkvs, dkvn = call(
        second_kernel,
        (shape((2, 512, HD)), shape((256, 256), F32)) + (shape((256, 256)),) * 4,
        (ids, qd1, qd3, *keys, kvn, dk, dv),
        smem=(0,),
        scratch=scratch(1280),
    )
    dq_core = swap(dq_send, 1)
    for m in (2, 1, 3):
        dkvs[m] = swap_y(dkvs[m], m)
    half, dq_sum = call(add_kernel, (shape((512, HD)), shape((512, HD), F32)), (dq_keep, dq_core))
    one_hot, noisy = call(
        prepare_kernel, (shape((RUNS, RUN, RUN)), shape((RUNS, RUN, 256))), (dkvn, copies)
    )
    back = call(
        unsort_kernel,
        shape((16, 3 * rows, HD)),
        (dq_sum, swap(half, 2), dkvs[0], dkvs[3], dkvs[2], dkvs[1], one_hot, noisy),
    )
    back = lax.all_to_all(back, BACK_AXES, 0, 0, tiled=True)
    return call(unpack_kernel, (shape((rows, 16 * HD)),) * 3, (back,))


def solution(mesh):
    fine = Mesh(mesh.devices.reshape(SIZES), AXES)
    whole = P(AXES, None)
    return jax.shard_map(
        per_device,
        mesh=fine,
        in_specs=(whole, whole, whole, whole, whole, P(AXES[:5], AXES[5]), P(), P()),
        out_specs=(whole, whole, whole),
        check_vma=False,
    )
```

```python
import jax
import jax.numpy as jnp
from jax import lax
from jax.experimental import pallas as pl
from jax.experimental.pallas import tpu as pltpu
from jax.sharding import Mesh
from jax.sharding import PartitionSpec as P

HD = 128
RUN = 128
HALF = RUN // 2
AXES = ("y", "zh", "xh", "xl", "c", "zl")
SIZES = (4, 2, 2, 2, 2, 4)
HEAD_AXES = ("zl", "zh", "xl")
BACK_AXES = ("zh", "xl", "zl")
QUERY_AXES = ("xh", "c")
RUNS = 4
SCALE = HD**-0.5
LOG2E = 1.4426950408889634
OFF = 1e30
F32 = jnp.float32
BF16 = jnp.bfloat16
VMEM = pl.BlockSpec(memory_space=pltpu.VMEM)
HBM = pl.BlockSpec(memory_space=pltpu.HBM)
SMEM = pl.BlockSpec(memory_space=pltpu.SMEM)


def iota(shape, axis):
    return lax.broadcasted_iota(jnp.int32, shape, axis)


def split_two(x):
    high = x.astype(BF16).astype(F32)
    return high, x - high


def contract(a, b, dim_a, dim_b):
    return lax.dot_general(a, b, (((dim_a,), (dim_b,)), ((), ())), preferred_element_type=F32)


def call(body, out_shape, args, smem=(), hbm=(), scratch=(), limit=32 << 20, cost=None):
    return pl.pallas_call(
        body,
        out_shape=out_shape,
        in_specs=[SMEM if i in smem else HBM if i in hbm else VMEM for i in range(len(args))],
        out_specs=jax.tree.map(lambda _: VMEM, out_shape),
        scratch_shapes=list(scratch),
        compiler_params=pltpu.CompilerParams(vmem_limit_bytes=limit),
        cost_estimate=cost,
    )(*args)


def pack_kernel(
    q_in, k_in, v_in, o_in, g_in, lse_in, copy_in, out_ref, there_ref, back_ref,
    q_ref, k_ref, v_ref, o_ref, g_ref, lse_ref, copy_ref, sems,
):
    pairs = ((copy_in, copy_ref), (g_in, g_ref), (o_in, o_ref), (lse_in, lse_ref), (q_in, q_ref), (k_in, k_ref), (v_in, v_ref))
    copies = [pltpu.make_async_copy(a, b, sems.at[i]) for i, (a, b) in enumerate(pairs)]
    for copy in copies:
        copy.start()
    rows = q_ref.shape[0]
    copies[0].wait()
    for j in range(RUNS):
        one_hot = placing(copy_ref, j)
        there_ref[j] = one_hot.astype(BF16)
        back_ref[j] = one_hot.T.astype(BF16)
    for copy in copies[1:4]:
        copy.wait()
    lane = iota((rows, 128), 1)
    delta = jnp.zeros((rows, 128), F32)
    for h in range(16):
        cols = slice(h * HD, (h + 1) * HD)
        term = g_ref[:, cols].astype(F32) * o_ref[:, cols].astype(F32)
        delta = jnp.where(lane == h, jnp.sum(term, axis=1, keepdims=True), delta)
    delta = jnp.concatenate([delta, jnp.zeros((128 - rows, 128), F32)], axis=0).T
    delta_high, delta_low = split_two(delta)
    lse_high, lse_low = split_two(lse_ref[...])
    row = iota((16, 128), 0)
    for copy in copies[4:]:
        copy.wait()
    for h in range(16):
        j = h % 4
        cols = slice(h * HD, (h + 1) * HD)
        for i, ref in enumerate((q_ref, g_ref, k_ref, v_ref)):
            out_ref[h, i * rows : (i + 1) * rows, :] = ref[:, cols]
        stats = jnp.where(row == 0, lse_high[j : j + 1], 0.0)
        stats = jnp.where(row == 1, lse_low[j : j + 1], stats)
        stats = jnp.where(row == 2, delta_high[h : h + 1], stats)
        stats = jnp.where(row == 3, delta_low[h : h + 1], stats)
        out_ref[h, 4 * rows : 4 * rows + 16, :] = stats.astype(BF16)


def placing(copy_ref, j):
    zh, xl = divmod(j, 2)
    shard = ((lax.axis_index("y") * 2 + zh) * 4 + lax.axis_index("xh") * 2 + xl) * 2 + lax.axis_index("c")
    copy = jnp.broadcast_to(copy_ref[pl.ds(shard, 1), :], (8, RUN)).astype(F32)
    upto = (iota((RUN, RUN), 0) <= iota((RUN, RUN), 1)).astype(BF16)
    count = contract(copy.astype(BF16), upto, 1, 0)
    index = iota((8, RUN), 1).astype(F32)
    place = jnp.where(copy > 0.5, HALF - 1.0 + count, index - count)
    place = jnp.broadcast_to(place[0:1], (RUN, RUN)).astype(jnp.int32)
    return (iota((RUN, RUN), 0) == place).astype(F32)


def sort_kernel(got_ref, there_ref, qd_ref, kv_ref, kvn_ref):
    zl = lax.axis_index("zl")
    row = iota((16, RUN), 0)
    stats = []
    for j in range(RUNS):
        zh, xl = divmod(j, 2)
        one_hot = there_ref[j]
        parts = [
            jnp.concatenate([got_ref[4 * z + j, 32 * i : 32 * i + 32, :] for z in range(4)], axis=0)
            for i in range(4)
        ]
        moved = contract(one_hot, jnp.concatenate(parts, axis=1), 1, 0).astype(BF16)
        qd_ref[256 * zh + 64 * xl : 256 * zh + 64 * xl + 64, :] = moved[:HALF, :256]
        qd_ref[256 * zh + 128 + 64 * xl : 256 * zh + 192 + 64 * xl, :] = moved[HALF:, :256]
        kvn_ref[128 * zh + 64 * xl : 128 * zh + 64 * xl + 64, :] = moved[:HALF, 256:]
        kv_ref[128 * zh + 64 * xl : 128 * zh + 64 * xl + 64, :] = moved[HALF:, 256:]
        lse = got_ref[4 * zl + j, 128:144, :].astype(F32)
        delta = jnp.concatenate(
            [got_ref[4 * z + j, 128:144, :].astype(F32)[:, :32] for z in range(4)], axis=1
        )
        both = jnp.where(row < 2, lse, delta).astype(BF16)
        stats.append(contract(both, one_hot, 1, 1))
    halves = []
    for zh in range(2):
        a, b = stats[2 * zh], stats[2 * zh + 1]
        halves.append(
            jnp.concatenate([a[:8, :HALF], b[:8, :HALF], a[:8, HALF:], b[:8, HALF:]], axis=1)
        )
    qd_ref[512:528, :] = jnp.concatenate(halves, axis=0).astype(BF16)


def load_keys(pieces, k_all, kt_all, v_all):
    for m, ref in enumerate(pieces):
        rows = slice(256 * m, 256 * m + 256)
        k = ref[:, :HD]
        k_all[rows, :] = k
        v_all[rows, :] = ref[:, HD:]
        kt_all[:, rows] = k.astype(F32).T.astype(BF16)


def attend(ids_ref, qd_ref, other, masks, noisy, k_all, kt_all, v_all):
    y, xh = lax.axis_index("y"), lax.axis_index("xh")
    stats = qd_ref[512:528, :].astype(F32)
    lse = jnp.concatenate([stats[0:1] + stats[1:2], stats[8:9] + stats[9:10]], axis=1) * LOG2E
    delta = jnp.concatenate([stats[2:3] + stats[3:4], stats[10:11] + stats[11:12]], axis=1)
    lane = iota((1, 512), 1)
    clean, second = lane // 128 % 2 == 1, lane >= 256
    own_ids = [ids_ref[(y * 2 + zh) * 2 + (xh ^ other)] for zh in range(2)]
    limits = []
    for mask in masks:
        for zh in range(2):
            key_id = ids_ref[((y ^ mask) * 2 + zh) * 2 + xh]
            noisy_off, clean_off = (
                jnp.where(second, *(jnp.where(hit, 0.0, OFF) for hit in hits))
                for hits in ([key_id < i for i in own_ids[::-1]], [key_id <= i for i in own_ids[::-1]])
            )
            limits.append(lse + jnp.where(clean, clean_off, noisy_off))
    if noisy:
        limits.append(lse + jnp.where(clean | second, OFF, 0.0))
        limits.append(lse + jnp.where(clean | ~second, OFF, 0.0))
    q, g = qd_ref[:512, :HD], qd_ref[:512, HD:]
    scores = contract(k_all, q, 1, 1)
    weights = jnp.concatenate(
        [jnp.exp2(scores[128 * i : 128 * i + 128] * (SCALE * LOG2E) - row) for i, row in enumerate(limits)], axis=0
    )
    dweights = contract(v_all, g, 1, 1)
    dscores = (weights * (dweights - delta)).astype(BF16)
    dv = contract(weights.astype(BF16), g, 1, 0)
    dk = contract(dscores, q, 1, 0)
    return dk, dv, contract(kt_all, dscores, 1, 0).T * SCALE


def own_kernel(ids_ref, qd0, kv0, kvn_ref, dq_ref, dk_ref, dv_ref, k_all, kt_all, v_all):
    load_keys((kv0, kvn_ref), k_all, kt_all, v_all)
    dk_ref[...], dv_ref[...], dq_ref[...] = attend(
        ids_ref, qd0, 0, (0,), True, k_all[...], kt_all[...], v_all[...]
    )


def first_kernel(
    ids_ref, qd0, qd2, kv0, kv1, kv2, kv3, own_dq, own_dk, own_dv, dq_ref, dk_ref, dv_ref, k_all, kt_all, v_all
):
    load_keys((kv0, kv1, kv2, kv3), k_all, kt_all, v_all)
    far_dk, far_dv, dq_ref[1] = attend(ids_ref, qd2, 1, range(4), False, k_all[...], kt_all[...], v_all[...])
    dk, dv, dq = attend(
        ids_ref, qd0, 0, (1, 2, 3), False, k_all[256:, :], kt_all[:, 256:], v_all[256:, :]
    )
    dq_ref[0] = own_dq[...] + dq
    for total, own, near, far in ((dk_ref, own_dk, dk, far_dk), (dv_ref, own_dv, dv, far_dv)):
        total[:256, :] = own[:256, :] + far[:256]
        total[256:1024, :] = near + far[256:]
        total[1024:, :] = own[256:, :]


def second_kernel(
    ids_ref, qd1, qd3, kv0, kv1, kv2, kv3, kvn_ref, dk_ref, dv_ref,
    dq_ref, dkv0, dkv1, dkv2, dkv3, dkvn, k_all, kt_all, v_all,
):
    load_keys((kv0, kv1, kv2, kv3, kvn_ref), k_all, kt_all, v_all)
    near_dk, near_dv, dq = attend(ids_ref, qd1, 0, range(4), True, k_all[...], kt_all[...], v_all[...])
    dq_ref[0] = dq.astype(BF16)
    far_dk, far_dv, dq = attend(
        ids_ref, qd3, 1, range(4), False, k_all[:1024, :], kt_all[:, :1024], v_all[:1024, :]
    )
    dq_ref[1] = dq.astype(BF16)
    for m, ref in enumerate((dkv0, dkv1, dkv2, dkv3, dkvn)):
        rows = slice(256 * m, 256 * m + 256)
        dk, dv = dk_ref[rows, :] + near_dk[rows], dv_ref[rows, :] + near_dv[rows]
        if m < 4:
            dk, dv = dk + far_dk[rows], dv + far_dv[rows]
        ref[:, :HD] = (dk * SCALE).astype(ref.dtype)
        ref[:, HD:] = dv.astype(ref.dtype)


def add_kernel(keep_ref, got_ref, send_ref, sum_ref):
    send_ref[...] = (keep_ref[1] + got_ref[1].astype(F32)).astype(BF16)
    sum_ref[...] = keep_ref[0] + got_ref[0].astype(F32)


def prepare_kernel(dkvn_ref, back_ref, noisy_ref):
    for j in range(RUNS):
        one_hot = back_ref[j]
        rows = dkvn_ref[64 * j : 64 * j + 64, :]
        noisy_ref[j] = contract(one_hot, jnp.concatenate([rows, jnp.zeros_like(rows)], axis=0), 1, 0).astype(BF16)


def unsort_kernel(sum_ref, got_chip, dkv0, dkv1, dkv2, dkv3, one_hot_ref, noisy_ref, out_ref):
    dq = (sum_ref[...] + got_chip[...].astype(F32)).astype(BF16)
    dkv = (dkv0[...] + dkv1[...].astype(F32) + dkv2[...].astype(F32) + dkv3[...].astype(F32)).astype(BF16)
    for j in range(RUNS):
        zh, xl = divmod(j, 2)
        at = 64 * xl
        queries = jnp.concatenate(
            [dq[256 * zh + at : 256 * zh + at + 64], dq[256 * zh + 128 + at : 256 * zh + 192 + at]], axis=0
        )
        rows = dkv[64 * j : 64 * j + 64]
        keys = jnp.concatenate([jnp.zeros_like(rows), rows], axis=0)
        moved = contract(one_hot_ref[j], jnp.concatenate([queries, keys], axis=1), 1, 0)
        moved_keys = (moved[:, HD:] + noisy_ref[j].astype(F32)).astype(BF16)
        moved = jnp.concatenate([moved[:, :HD].astype(BF16), moved_keys], axis=1)
        for z in range(4):
            for i in range(3):
                out_ref[4 * j + z, 32 * i : 32 * i + 32, :] = moved[32 * z : 32 * z + 32, HD * i : HD * (i + 1)]


def unpack_kernel(got_ref, dq_ref, dk_ref, dv_ref):
    rows = dq_ref.shape[0]
    for h in range(16):
        for i, ref in enumerate((dq_ref, dk_ref, dv_ref)):
            ref[:, h * HD : (h + 1) * HD] = got_ref[4 * (h % 4) + h // 4, i * rows : (i + 1) * rows, :]


def swap(x, mask):
    return lax.ppermute(x, QUERY_AXES, [(i, i ^ mask) for i in range(4)])


def swap_y(x, mask):
    return lax.ppermute(x, "y", [(i, i ^ mask) for i in range(4)])


def shape(dims, dtype=BF16):
    return jax.ShapeDtypeStruct(dims, dtype)


def per_device(query_in, key_in, value_in, saved_out, grad_out, saved_lse, row_block, row_copy):
    copies = row_copy.reshape(-1, RUN)
    ids = row_block[:: 4 * RUN]
    rows = query_in.shape[0]
    arrays = (query_in, key_in, value_in, saved_out, grad_out, saved_lse.T, copies)
    packed, there, back_places = call(
        pack_kernel,
        (shape((16, 4 * rows + 16, HD)),) + (shape((RUNS, RUN, RUN)),) * 2,
        tuple(pltpu.with_memory_space_constraint(x, pltpu.HBM) for x in arrays),
        hbm=range(7),
        scratch=[pltpu.VMEM(query_in.shape, BF16)] * 5 + [
            pltpu.VMEM((4, 128), F32), pltpu.VMEM(copies.shape, copies.dtype), pltpu.SemaphoreType.DMA((7,))
        ],
    )
    got = lax.all_to_all(packed, HEAD_AXES, 0, 0, tiled=True)
    qd, kv, kvn = call(
        sort_kernel, (shape((528, 256)), shape((256, 256)), shape((256, 256))), (got, there)
    )
    qd2 = swap(qd, 2)
    kv3, kv2, kv1 = (swap_y(kv, m) for m in (3, 2, 1))
    def scratch(count):
        return pltpu.VMEM((count, HD), BF16), pltpu.VMEM((HD, count), BF16), pltpu.VMEM((count, HD), BF16)

    part = shape((512, HD), F32)
    own = call(own_kernel, (part,) * 3, (ids, qd, kv, kvn), smem=(0,), scratch=scratch(512))
    qd2, kv3, kv2, kv1, ids, qd, *own = lax.optimization_barrier((qd2, kv3, kv2, kv1, ids, qd, *own))
    qd1 = swap(qd, 1)
    qd3 = swap(qd2, 1)
    keys = (kv, kv1, kv2, kv3)
    total = shape((1280, HD), F32)
    dq_keep, dk, dv = call(
        first_kernel,
        (shape((2, 512, HD), F32), total, total),
        (ids, qd, qd2, *keys, *own),
        smem=(0,),
        scratch=scratch(1024),
    )
    dq_send, *dkvs, dkvn = call(
        second_kernel,
        (shape((2, 512, HD)), shape((256, 256), F32)) + (shape((256, 256)),) * 4,
        (ids, qd1, qd3, *keys, kvn, dk, dv),
        smem=(0,),
        scratch=scratch(1280),
    )
    dq_core = swap(dq_send, 1)
    for m in (2, 1, 3):
        dkvs[m] = swap_y(dkvs[m], m)
    half, dq_sum = call(add_kernel, (shape((512, HD)), shape((512, HD), F32)), (dq_keep, dq_core))
    noisy = call(prepare_kernel, shape((RUNS, RUN, 256)), (dkvn, back_places))
    back = call(
        unsort_kernel,
        shape((16, 3 * rows, HD)),
        (dq_sum, swap(half, 2), dkvs[0], dkvs[3], dkvs[2], dkvs[1], back_places, noisy),
    )
    back = lax.all_to_all(back, BACK_AXES, 0, 0, tiled=True)
    return call(unpack_kernel, (shape((rows, 16 * HD)),) * 3, (back,))


def solution(mesh):
    fine = Mesh(mesh.devices.reshape(SIZES), AXES)
    whole = P(AXES, None)
    return jax.shard_map(
        per_device,
        mesh=fine,
        in_specs=(whole, whole, whole, whole, whole, P(AXES[:5], AXES[5]), P(), P()),
        out_specs=(whole, whole, whole),
        check_vma=False,
    )
```
